32 devices in a mesh: groups: 2 (over y), req: 4 (over z), tensor: 4 (over x, core).
Axes of the slice: x: 2, y: 2, z: 4, core: 2. Of those that a mesh axis runs over, the one named last changes fastest.
Arguments:
- tokens: bfloat16 [2048, 5120], P(('groups', 'req')), parts along dimension 0, may hold values from -6 to 6
- w_x: bfloat16 [5120, 4096], P('req', 'tensor'), may hold values from -0.078125 to 0.078125
- w_bc: bfloat16 [5120, 256], P('req'), may hold values from -0.0078125 to 0.0078125
- w_dt: bfloat16 [5120, 64], P('req', 'tensor'), may hold values from -0.078125 to 0.078125
- dt_bias: float32 [64], P('tensor'), may hold values from -2 to 0.5
- decay_rate: float32 [64], P('tensor'), may hold values from 0.004 to 1
- skip_gain: float32 [64], P('tensor'), may hold values from 0.3 to 1.5
- w_out: bfloat16 [4096, 5120], P('tensor', 'req'), may hold values from -0.09375 to 0.09375
- suffix_lengths: int32 [8, 8], P(('groups', 'req')), parts along dimension 0, may hold values from 1 to 96, 256 in all within a row
- checkpoint_slot: int32 [64], P('groups'), parts along dimension 0, may hold values from 0 to 47, as said below
- cache: float32 [96, 64, 64, 128], P(('groups', 'req'), 'tensor'), parts along dimension 0, may hold values from -6 to 6
Outputs:
- layer_out: bfloat16 [2048, 5120], P(('groups', 'req'), 'tensor'), parts along dimension 0
- new_cache: float32 [96, 64, 64, 128], P(('groups', 'req'), 'tensor'), parts along dimension 0
The draws below stay inside these ranges and needn't reach their ends.
There are 2 independent parts, one for each index of `groups`. The reference program is written for one: setup_inputs(seed, part) draws one part's arguments, and reference() takes and returns one part's arrays. A program takes and returns all parts, laid end to end along the dimension named above; an argument that names none is the same for every part. Nothing has to cross between parts.
Inputs may be any that keep to these rules, and one draw needn't show every extreme that they name: `checkpoint_slot`: entries are distinct. Slot k lies on req index k // 12. At most 3 requests of one req index have their checkpoints on one req index, and this is reached in every draw; some req index has all its 12 slots in use. `suffix_lengths`: each row sums to 256.
All inputs are finite; a program needn't handle non-finite values.
Results may differ from the reference program's by a relative error of at most 0.013.
Values may be sent and summed in bfloat16 or wider, within the bound.
No kernel may reach another device: no remote copies, remote signals or barrier semaphores. Data moves between devices by JAX's collectives and lax.ppermute only.
A program may use at most 128 MiB of HBM per device.

```python
import math
import jax
import jax.numpy as jnp
import numpy as np
from jax import lax

D = 5120
SSM_HEADS = 64
HEAD_P = 64
D_STATE = 128
TOK_DEV = 256
REQ_DEV = 8
REQ_SHARDS = 4
SLOTS_DEV = 12
REQS = 32
TOKENS = 1024
SLOTS = 48
N_TENSOR = 4


def draw_checkpoint_slot(key, part):
    key = jax.random.fold_in(key, 7)
    keys = jax.random.split(key, 5)
    holders = REQ_SHARDS
    leaning = jax.random.randint(keys[0], (holders,), 0, 4)
    chosen = jax.random.randint(keys[1], (), 0, holders)
    leaning = jnp.where(jnp.arange(holders) == chosen, 16, leaning)
    noise = jax.random.randint(keys[2], (SLOTS,), 0, 512)
    places = jnp.arange(SLOTS, dtype=jnp.int32)
    score = (leaning[places // SLOTS_DEV] * 512 + noise) * SLOTS + places
    picked = jnp.sort(lax.top_k(score, REQS)[1].astype(jnp.int32))
    rotate = jax.random.randint(keys[3], (), 0, holders)
    order = jnp.arange(REQS, dtype=jnp.int32)
    owner = (order + rotate) % holders
    within_rank = order // holders
    shuffle = jnp.argsort(jax.random.randint(keys[4], (holders, REQ_DEV), 0, 1 << 20) * REQ_DEV + jnp.arange(REQ_DEV, dtype=jnp.int32)[None, :], axis=1).astype(jnp.int32)
    within = shuffle[owner, within_rank]
    table = jnp.zeros((REQS,), jnp.int32).at[owner * REQ_DEV + within].set(picked)
    return table


def level_of(stream_key, dims, shards, least, largest):
    gain = 1.0
    for dim, shards_of in shards:
        steps = jax.random.uniform(jax.random.fold_in(jax.random.fold_in(stream_key, 6), dim), (shards_of,), jnp.float32, least / len(shards), largest / len(shards))
        gain = gain * jnp.repeat(jnp.exp(steps), dims[dim] // shards_of).reshape((-1,) + (1,) * (len(dims) - 1 - dim))
    return gain


def length_profile(amount, total, limit, lean):
    loads = [(1 << 20) // math.isqrt(rank ** lean) + 1 for rank in range(2, amount + 1)]
    rest, given = total - limit - (amount - 1), [1] * (amount - 1)
    while rest > 0:
        movable = [i for i in range(amount - 1) if given[i] < limit]
        mass, left = sum([loads[i] for i in movable]), rest
        for i in movable:
            addition = min(limit - given[i], max(1, left * loads[i] // mass), rest)
            given[i] = given[i] + addition
            rest = rest - addition
    return np.array([limit] + given)


def uneven(own_key, amount, total, most, lean):
    if amount == 2:
        one = jax.random.randint(own_key, (), max(1, total - most), min(most, total - 1) + 1)
        return jnp.stack([one, total - one])
    sizes = jnp.asarray(length_profile(amount, total, most, lean), jnp.int32)
    couples = (amount - 1) // 2
    giver, taker = sizes[1:1 + 2 * couples:2], sizes[2:2 + 2 * couples:2]
    slack = jnp.minimum(giver - 1, most - taker)
    shifted = jax.random.randint(jax.random.fold_in(own_key, 1), (couples,), 0, 1 << 20) % (slack + 1)
    sizes = sizes.at[1:1 + 2 * couples:2].set(giver - shifted).at[2:2 + 2 * couples:2].set(taker + shifted)
    return sizes[jax.random.permutation(jax.random.fold_in(own_key, 2), amount)]


def bell_draw(rng, extent, deviation, limit, shards=(), kind=jnp.bfloat16):
    result = deviation * jax.random.normal(rng, extent, jnp.float32)
    if shards:
        result = result * level_of(rng, extent, shards, -0.22, 0.18)
    return jnp.clip(result, -limit, limit).astype(kind)


def setup_inputs(seed: int = 0, part: int = 0) -> dict:
    key_of = jax.random.split(jax.random.key(seed), 12)
    part_keys = jax.random.split(jax.random.fold_in(key_of[11], part), 12)
    tokens = bell_draw(part_keys[0], (TOKENS, D), 1.0, 6.0, ((0, 4),))
    w_x = bell_draw(key_of[1], (D, SSM_HEADS * HEAD_P), D ** -0.5, 0.078125, ((0, 4), (1, 4)))
    w_bc = bell_draw(key_of[2], (D, 2 * D_STATE), (D * D_STATE) ** -0.5, 0.0078125, ((0, 4),))
    w_dt = bell_draw(key_of[3], (D, SSM_HEADS), D ** -0.5, 0.078125, ((0, 4), (1, 4)))
    dt_bias = jnp.clip(-2.0 + 2.5 * jax.random.uniform(key_of[4], (SSM_HEADS,), jnp.float32) ** level_of(key_of[4], (SSM_HEADS,), ((0, 4),), -0.2, 0.2), -2.0, 0.5)
    decay_rate = jnp.clip(jnp.exp(math.log(1.0) - 5.521461 * jax.random.uniform(key_of[5], (SSM_HEADS,), jnp.float32) ** level_of(key_of[5], (SSM_HEADS,), ((0, 4),), -0.2, 0.2)), 0.004, 1.0)
    skip_gain = jnp.clip(0.3 + 1.2 * jax.random.uniform(key_of[6], (SSM_HEADS,), jnp.float32) ** level_of(key_of[6], (SSM_HEADS,), ((0, 4),), -0.2, 0.2), 0.3, 1.5)
    w_out = bell_draw(key_of[7], (SSM_HEADS * HEAD_P, D), (SSM_HEADS * HEAD_P) ** -0.5, 0.09375, ((0, 4), (1, 4)))
    suffix_lengths = jax.vmap(lambda own: uneven(own, REQ_DEV, TOK_DEV, 3 * TOK_DEV // REQ_DEV, 2))(jax.random.split(part_keys[8], REQ_SHARDS)).reshape((REQ_SHARDS, REQ_DEV)).astype(jnp.int32)
    checkpoint_slot = draw_checkpoint_slot(jax.random.fold_in(jax.random.fold_in(key_of[11], part), 71), part)
    cache = bell_draw(part_keys[10], (SLOTS, SSM_HEADS, HEAD_P, D_STATE), 1.0, 6.0, ((0, 4), (1, 4)), jnp.float32)
    return {"tokens": tokens, "w_x": w_x, "w_bc": w_bc, "w_dt": w_dt, "dt_bias": dt_bias, "decay_rate": decay_rate, "skip_gain": skip_gain, "w_out": w_out, "suffix_lengths": suffix_lengths, "checkpoint_slot": checkpoint_slot, "cache": cache}


HIGH = lax.Precision.HIGHEST


def suffix_scan(inputs_ssm, state_maps, step_size, decay_rate, skip_gain, lengths, initial):
    num_tok = inputs_ssm.shape[0]
    state_dim = state_maps.shape[1] // 2
    head_count = step_size.shape[1]
    head_width = inputs_ssm.shape[1] // head_count
    places = jnp.arange(num_tok, dtype=jnp.int32)
    seg_end = jnp.cumsum(lengths).astype(jnp.int32)
    starts = seg_end - lengths
    member = ((places[:, None] >= starts[None, :]) & (places[:, None] < seg_end[None, :])).astype(jnp.float32)
    same_seg = jnp.dot(member, member.T, precision=HIGH)
    causal = same_seg * (places[:, None] >= places[None, :]).astype(jnp.float32)
    log_decay = -step_size * decay_rate[None, :]
    running = jnp.dot(causal, log_decay, precision=HIGH)
    totals = jnp.dot(member.T, log_decay, precision=HIGH)
    b_part = state_maps[:, :state_dim]
    c_part = state_maps[:, state_dim:]
    scores = jnp.dot(c_part, b_part.T, precision=HIGH)
    spread = jnp.minimum(running[:, None, :] - running[None, :, :], 0.0)
    mixing = jnp.where(causal[:, :, None] > 0, jnp.exp(spread), 0.0) * scores[:, :, None] * step_size[None, :, :]
    mixing = lax.optimization_barrier(mixing.astype(jnp.bfloat16)).astype(jnp.float32)
    values = inputs_ssm.reshape(num_tok, head_count, head_width).astype(jnp.float32)
    within = jnp.einsum("tsh,shp->thp", mixing, values, precision=HIGH)
    from_cache = jnp.einsum("tn,rhpn->trhp", c_part, initial, precision=HIGH)
    carried = jnp.einsum("tr,trhp->thp", member, from_cache, precision=HIGH)
    outputs = within + jnp.exp(running)[:, :, None] * carried + skip_gain[None, :, None] * values
    weights = jnp.where(member[:, :, None] > 0, jnp.exp(jnp.minimum(totals[None, :, :] - running[:, None, :], 0.0)), 0.0) * step_size[:, None, :]
    scaled = weights[:, :, :, None] * values[:, None, :, :]
    increment = jnp.einsum("trhp,tn->rhpn", scaled, b_part, precision=HIGH)
    new_states = jnp.exp(totals)[:, :, None, None] * initial + increment
    return outputs.astype(jnp.bfloat16).reshape(num_tok, head_count * head_width), new_states


def reference(tokens, w_x, w_bc, w_dt, dt_bias, decay_rate, skip_gain, w_out, suffix_lengths, checkpoint_slot, cache):
    inputs_ssm = jnp.dot(tokens, w_x, preferred_element_type=jnp.float32).astype(jnp.bfloat16)
    state_maps = jnp.dot(tokens, w_bc, preferred_element_type=jnp.float32)
    step_size = jax.nn.softplus(jnp.dot(tokens, w_dt, preferred_element_type=jnp.float32) + dt_bias[None, :])
    initial = jnp.take(cache, checkpoint_slot, axis=0)
    width_all = SSM_HEADS * HEAD_P

    def per_owner(items):
        return suffix_scan(items[0], items[1], items[2], decay_rate, skip_gain, items[3], items[4])

    outputs, new_states = lax.map(per_owner, (
        inputs_ssm.reshape(REQ_SHARDS, TOK_DEV, width_all),
        state_maps.reshape(REQ_SHARDS, TOK_DEV, 2 * D_STATE),
        step_size.reshape(REQ_SHARDS, TOK_DEV, SSM_HEADS),
        suffix_lengths,
        initial.reshape(REQ_SHARDS, REQ_DEV, SSM_HEADS, HEAD_P, D_STATE)))
    outputs = outputs.reshape(TOKENS, width_all)
    block_width = width_all // N_TENSOR
    summed = jnp.zeros((TOKENS, D), jnp.float32)
    for part_index in range(N_TENSOR):
        lower = part_index * block_width
        partial_value = jnp.dot(outputs[:, lower:lower + block_width], w_out[lower:lower + block_width], preferred_element_type=jnp.float32)
        partial_value = lax.optimization_barrier(partial_value.astype(jnp.bfloat16)).astype(jnp.float32)
        summed = summed + partial_value
    new_cache = cache.at[checkpoint_slot].set(new_states.reshape(REQS, SSM_HEADS, HEAD_P, D_STATE))
    return summed.astype(jnp.bfloat16), new_cache
```

```python
import functools

import jax
import jax.numpy as jnp
from jax import lax
from jax.experimental import pallas as pl
from jax.experimental.pallas import tpu as pltpu
from jax.sharding import PartitionSpec as P

HIGH = lax.Precision.HIGHEST
BF = jnp.bfloat16
F32 = jnp.float32
NT = (((1,), (1,)), ((), ()))
TN = (((0,), (0,)), ((), ()))


def params():
    return pltpu.CompilerParams(vmem_limit_bytes=48 * 1024 * 1024)


def exchange(x, axis="req"):
    return lax.all_to_all(x, axis, split_axis=0, concat_axis=0, tiled=True)


def spread_out(x, axis="req"):
    count = lax.axis_size(axis)
    return exchange(jnp.broadcast_to(x[None], (count,) + x.shape), axis)


def swap_core(x):
    count = lax.axis_size("tensor")
    return lax.ppermute(x, "tensor", [(i, i ^ 1) for i in range(count)])


def chip_turn(x, turn):
    count = lax.axis_size("tensor")
    return lax.ppermute(x, "tensor", [(i, (i + 2 * turn) % count) for i in range(count)])


def sum_tensor(x):
    x = x + swap_core(x)
    total = x
    for turn in range(1, lax.axis_size("tensor") // 2):
        total = total + chip_turn(x, turn)
    return total


def carried_kernel(slot, start, stop, c_ref, *refs):
    *states, out = refs
    owner = pl.program_id(0)
    rows = lax.broadcasted_iota(jnp.int32, (c_ref.shape[1], 1), 0)
    c_part = c_ref[0]
    total = jnp.zeros(out.shape[1:], F32)
    for rank, state in enumerate(states):
        at = owner * len(states) + rank
        inside = (rows >= start[at]) & (rows < stop[at])
        mine = jnp.where(inside, c_part, jnp.zeros_like(c_part))
        heads, width, dim = state.shape[1:]
        flat = state[0].reshape(heads * width, dim).astype(BF)
        total += lax.dot_general(mine, flat, NT, preferred_element_type=F32)
    out[0] = total.astype(BF)


def carried_part(slot, start, stop, c_all, cache, per_pair):
    owners, num_tok, dim = c_all.shape
    _, heads, width, _ = cache.shape

    def state_map(rank, o, slot, start, stop):
        return (slot[o * per_pair + rank], 0, 0, 0)

    return pl.pallas_call(
        carried_kernel,
        out_shape=jax.ShapeDtypeStruct((owners, num_tok, heads * width), BF),
        grid_spec=pltpu.PrefetchScalarGridSpec(
            num_scalar_prefetch=3,
            grid=(owners,),
            in_specs=[pl.BlockSpec((1, num_tok, dim), lambda o, *_: (o, 0, 0))]
            + [
                pl.BlockSpec((1, heads, width, dim), functools.partial(state_map, rank))
                for rank in range(per_pair)
            ],
            out_specs=pl.BlockSpec((1, num_tok, heads * width), lambda o, *_: (o, 0, 0)),
        ),
        compiler_params=params(),
        cost_estimate=pl.CostEstimate(
            flops=2 * owners * num_tok * dim * heads * width * per_pair,
            bytes_accessed=cache.size * 4 + owners * num_tok * heads * width * 2,
            transcendentals=0,
        ),
    )(slot, start, stop, c_all, *([cache] * per_pair))


def outputs_kernel(
    parts, carried, b_ref, c_ref, seg_row, seg_col, run_ref, run_t, step_t, gain, out, x_out, scores
):
    num_tok = b_ref.shape[0]

    @pl.when(pl.program_id(0) == 0)
    def _():
        raw = lax.dot_general(c_ref[...], b_ref[...], NT, preferred_element_type=F32)
        down = lax.broadcasted_iota(jnp.int32, (num_tok, num_tok), 0)
        along = lax.broadcasted_iota(jnp.int32, (num_tok, num_tok), 1)
        keep = (seg_row[...] == seg_col[...]) & (down >= along)
        scores[...] = jnp.where(keep, raw, 0.0)

    values = parts[0].astype(F32)
    for i in range(1, parts.shape[0]):
        values += parts[i].astype(F32)
    values = values.astype(BF)
    x_out[...] = values
    held = carried[0].astype(F32)
    for i in range(1, carried.shape[0]):
        held += carried[i].astype(F32)
    pair = run_ref.shape[2]
    width = values.shape[1] // pair
    lane = lax.broadcasted_iota(jnp.int32, values.shape, 1) // width
    total = jnp.zeros(values.shape, F32)
    grown = jnp.zeros(values.shape, F32)
    gains = jnp.zeros((1, values.shape[1]), F32)
    for i in range(pair):
        run_col = run_ref[0, :, i : i + 1]
        run_row = run_t[0, i : i + 1, :]
        step_row = step_t[0, i : i + 1, :]
        decay = jnp.exp(jnp.minimum(run_col - run_row, 0.0))
        mixing = (decay * scores[...] * step_row).astype(BF)
        within = jnp.dot(mixing, values, preferred_element_type=F32)
        total = jnp.where(lane == i, within, total)
        grown = jnp.where(lane == i, jnp.exp(run_col), grown)
        gains = jnp.where(lane[:1] == i, gain[0, :, i : i + 1], gains)
    out[...] = (total + grown * held + gains * values.astype(F32)).astype(BF)


def outputs_part(parts, carried, b_part, c_part, seg, running, step_size, gain):
    owners, num_tok, columns = parts.shape
    heads = running.shape[1]
    dim = b_part.shape[1]
    pair = 2
    steps = heads // pair
    lanes = columns // steps
    run_p = running.reshape(num_tok, steps, pair).transpose(1, 0, 2)
    run_t = running.T.reshape(steps, pair, num_tok)
    step_t = step_size.T.reshape(steps, pair, num_tok)

    def whole(*shape):
        return pl.BlockSpec(shape, lambda i: (0,) * len(shape))

    def per_step(*shape):
        return pl.BlockSpec((1,) + shape, lambda i: (i, 0, 0))

    wide = pl.BlockSpec((owners, num_tok, lanes), lambda i: (0, 0, i))
    slab = pl.BlockSpec((num_tok, lanes), lambda i: (0, i))
    return pl.pallas_call(
        outputs_kernel,
        out_shape=[jax.ShapeDtypeStruct((num_tok, columns), BF)] * 2,
        grid=(steps,),
        in_specs=[
            wide,
            wide,
            whole(num_tok, dim),
            whole(num_tok, dim),
            whole(num_tok, 1),
            whole(1, num_tok),
            per_step(num_tok, pair),
            per_step(pair, num_tok),
            per_step(pair, num_tok),
            per_step(1, pair),
        ],
        out_specs=[slab, slab],
        scratch_shapes=[pltpu.VMEM((num_tok, num_tok), F32)],
        compiler_params=params(),
        cost_estimate=pl.CostEstimate(
            flops=2 * num_tok * num_tok * columns * 2,
            bytes_accessed=parts.size * 4 + num_tok * columns * 4,
            transcendentals=num_tok * num_tok * heads,
        ),
    )(
        parts,
        carried,
        b_part,
        c_part,
        seg[:, None],
        seg[None, :],
        run_p,
        run_t,
        step_t,
        gain.reshape(steps, 1, pair),
    )


def states_kernel(owner, start, stop, state, x_ref, b_ref, run_ref, step_ref, out):
    at = pl.program_id(0)
    num_tok, heads = run_ref.shape[1:]
    width = state.shape[2]
    rows = lax.broadcasted_iota(jnp.int32, (num_tok, 1), 0)
    inside = (rows >= start[at]) & (rows < stop[at])
    last = rows == stop[at] - 1
    running = run_ref[0]
    totals = jnp.sum(jnp.where(last, running, 0.0), axis=0, keepdims=True)
    weights = jnp.where(inside, jnp.exp(jnp.minimum(totals - running, 0.0)), 0.0) * step_ref[0]
    head = lax.broadcasted_iota(jnp.int32, (heads, heads * width), 0)
    lane = lax.broadcasted_iota(jnp.int32, (heads, heads * width), 1) // width
    widen = (head == lane).astype(BF)
    wide = jnp.dot(weights.astype(BF), widen, preferred_element_type=F32)
    scaled = (x_ref[0].astype(F32) * wide).astype(BF)
    increment = lax.dot_general(scaled, b_ref[0], TN, preferred_element_type=F32)
    grown = jnp.exp(totals)
    for h in range(heads):
        out[0, h] = state[0, h] * grown[:, h : h + 1] + increment[h * width : (h + 1) * width]


def states_part(owner, start, stop, cache, x_all, b_all, run_all, step_all):
    slots, heads, width, dim = cache.shape
    _, num_tok, columns = x_all.shape

    def own(*shape):
        return pl.BlockSpec((1,) + shape, lambda s, owner, *_: (owner[s], 0, 0))

    slab = pl.BlockSpec((1, heads, width, dim), lambda s, *_: (s, 0, 0, 0))
    return pl.pallas_call(
        states_kernel,
        out_shape=jax.ShapeDtypeStruct(cache.shape, cache.dtype),
        grid_spec=pltpu.PrefetchScalarGridSpec(
            num_scalar_prefetch=3,
            grid=(slots,),
            in_specs=[
                slab,
                own(num_tok, columns),
                own(num_tok, dim),
                own(num_tok, heads),
                own(num_tok, heads),
            ],
            out_specs=slab,
        ),
        compiler_params=params(),
        cost_estimate=pl.CostEstimate(
            flops=2 * slots * num_tok * columns * dim,
            bytes_accessed=cache.size * 8 + slots * num_tok * columns * 2,
            transcendentals=slots * num_tok * heads,
        ),
    )(owner, start, stop, cache, x_all, b_all, run_all, step_all)


def body(
    tokens,
    w_x,
    w_bc,
    w_dt,
    dt_bias,
    decay_rate,
    skip_gain,
    w_out,
    suffix_lengths,
    checkpoint_slot,
    cache,
):
    reqs = lax.axis_size("req")
    tensors = lax.axis_size("tensor")
    chips = tensors // 2
    own_req = lax.axis_index("req")
    own_tensor = lax.axis_index("tensor")
    core = own_tensor % 2
    num_tok = tokens.shape[0]
    depth = w_x.shape[0]
    slots_dev, heads, width, state_dim = cache.shape
    columns = heads * width

    half = depth // 2
    outgoing = lax.dynamic_index_in_dim(
        tokens.reshape(num_tok, reqs, 2, half), core, axis=2, keepdims=False
    ).transpose(1, 0, 2)
    near = exchange(outgoing).reshape(reqs * num_tok, half)

    share = depth // tensors
    bc_rows = spread_out(lax.dynamic_slice_in_dim(w_bc, own_tensor * share, share))
    bc_tokens = lax.dynamic_index_in_dim(
        tokens.reshape(num_tok, reqs, tensors, share), own_tensor, axis=2, keepdims=False
    )
    state_maps = sum_tensor(
        jnp.dot(
            bc_tokens.reshape(num_tok, reqs * share),
            bc_rows.reshape(reqs * share, -1),
            preferred_element_type=F32,
        )
    ).astype(BF)
    b_part, c_part = state_maps[:, :state_dim], state_maps[:, state_dim:]
    c_all = spread_out(c_part)

    dt_rows = spread_out(w_dt.T)
    raw_step = jnp.einsum(
        "trk,rhk->th",
        tokens.reshape(num_tok, reqs, depth),
        dt_rows,
        preferred_element_type=F32,
    )
    step_size = jax.nn.softplus(raw_step + dt_bias[None, :])
    lengths = lax.all_gather(suffix_lengths[0], "req", axis=0)
    ends = jnp.cumsum(lengths, axis=1)
    begins = ends - lengths
    places = jnp.arange(num_tok, dtype=jnp.int32)
    own_ends = jnp.cumsum(suffix_lengths[0])
    seg = jnp.sum((places[:, None] >= own_ends[None, :]).astype(jnp.int32), axis=1)
    causal = ((seg[:, None] == seg[None, :]) & (places[:, None] >= places[None, :])).astype(F32)
    running = jnp.dot(causal, -step_size * decay_rate[None, :], precision=HIGH)
    timing = spread_out(jnp.concatenate([running, step_size], axis=1))
    b_all = spread_out(b_part)

    per_pair = (slots_dev + reqs - 1) // reqs
    total_reqs = checkpoint_slot.shape[0]
    req_dev = total_reqs // reqs
    holder = checkpoint_slot // slots_dev
    owner = jnp.arange(total_reqs, dtype=jnp.int32) // req_dev
    pair_key = holder * reqs + owner
    rank_in_pair = jnp.sum(
        (pair_key[:, None] == pair_key[None, :])
        & (checkpoint_slot[None, :] < checkpoint_slot[:, None]),
        axis=1,
    )
    slot_local = checkpoint_slot % slots_dev
    begin = begins.reshape(-1)
    end = ends.reshape(-1)
    pairs = jnp.arange(reqs * per_pair, dtype=jnp.int32)
    mine = holder == own_req
    match = mine[None, :] & ((owner * per_pair + rank_in_pair)[None, :] == pairs[:, None])

    def pick(match, values):
        return jnp.sum(jnp.where(match, values[None, :], 0), axis=1)

    carried = carried_part(
        pick(match, slot_local), pick(match, begin), pick(match, end), c_all, cache, per_pair
    )
    carried = exchange(carried)

    w_near = lax.dynamic_slice_in_dim(w_x, core * half, half)
    w_far = lax.dynamic_slice_in_dim(w_x, (1 - core) * half, half)
    far = swap_core(near)
    partial = jnp.dot(near, w_near, preferred_element_type=F32) + jnp.dot(
        far, w_far, preferred_element_type=F32
    )
    parts = exchange(partial.astype(BF).reshape(reqs, num_tok, columns))

    outputs, values = outputs_part(
        parts, carried, b_part, c_part, seg, running, step_size, skip_gain
    )
    all_outputs = spread_out(outputs).reshape(reqs * num_tok, columns)
    x_all = spread_out(values)

    product = jnp.dot(all_outputs, w_out, preferred_element_type=F32).astype(BF)
    rows_half = num_tok // 2
    out_columns = w_out.shape[1]
    product = product.reshape(reqs, 2, rows_half, out_columns)
    kept = lax.dynamic_index_in_dim(product, core, axis=1, keepdims=False)
    given = lax.dynamic_index_in_dim(product, 1 - core, axis=1, keepdims=False)
    summed = (kept.astype(F32) + swap_core(given).astype(F32)).astype(BF)
    arrived = exchange(summed).reshape(chips, 2, rows_half, out_columns)
    own_chip = own_tensor // 2
    total = lax.dynamic_index_in_dim(arrived, own_chip, axis=0, keepdims=False).astype(F32)
    for turn in range(1, chips):
        to_chip = (own_chip + turn) % chips
        given = lax.dynamic_index_in_dim(arrived, to_chip, axis=0, keepdims=False)
        total = total + chip_turn(given, turn).astype(F32)
    total = total.astype(BF)
    kept = lax.dynamic_index_in_dim(total, core, axis=0, keepdims=False)
    other = swap_core(lax.dynamic_index_in_dim(total, 1 - core, axis=0, keepdims=False))
    low = jnp.where(core == 0, kept, other)
    high = jnp.where(core == 0, other, kept)
    layer_out = jnp.concatenate([low, high], axis=0)

    slot_ids = own_req * slots_dev + jnp.arange(slots_dev, dtype=jnp.int32)
    match_slot = checkpoint_slot[None, :] == slot_ids[:, None]
    new_cache = states_part(
        pick(match_slot, owner),
        pick(match_slot, begin),
        pick(match_slot, end),
        cache,
        x_all,
        b_all,
        timing[:, :, :heads],
        timing[:, :, heads:],
    )
    return (layer_out, new_cache)


def solution(mesh):
    placed = (
        P(("groups", "req"), None),
        P("req", "tensor"),
        P("req", None),
        P("req", "tensor"),
        P("tensor"),
        P("tensor"),
        P("tensor"),
        P("tensor", "req"),
        P(("groups", "req"), None),
        P("groups"),
        P(("groups", "req"), "tensor", None, None),
    )
    return jax.shard_map(
        body,
        mesh=mesh,
        in_specs=placed,
        out_specs=(P(("groups", "req"), "tensor"), P(("groups", "req"), "tensor", None, None)),
        check_vma=False,
    )
```

```python
import functools

import jax
import jax.numpy as jnp
from jax import lax
from jax.experimental import pallas as pl
from jax.experimental.pallas import tpu as pltpu
from jax.sharding import PartitionSpec as P

HIGH = lax.Precision.HIGHEST
BF = jnp.bfloat16
F32 = jnp.float32
NN = (((1,), (0,)), ((), ()))
NT = (((1,), (1,)), ((), ()))
TN = (((0,), (0,)), ((), ()))
LANES = 128


def turn_req(x, turn):
    count = lax.axis_size("req")
    return lax.ppermute(x, "req", [(i, (i + turn) % count) for i in range(count)])


def swap_core(x):
    count = lax.axis_size("tensor")
    return lax.ppermute(x, "tensor", [(i, i ^ 1) for i in range(count)])


def turn_chip(x, turn):
    count = lax.axis_size("tensor")
    return lax.ppermute(x, "tensor", [(i, (i + 2 * turn) % count) for i in range(count)])


def spread_out(x):
    count = lax.axis_size("req")
    wide = jnp.broadcast_to(x[None], (count,) + x.shape)
    return lax.all_to_all(wide, "req", split_axis=0, concat_axis=0, tiled=True)


def sum_tensor(x):
    x = x + swap_core(x)
    total = x
    for turn in range(1, lax.axis_size("tensor") // 2):
        total = total + turn_chip(x, turn)
    return total


def dot32(a, b, dims):
    return lax.dot_general(a, b, dims, precision=HIGH, preferred_element_type=F32)


def dot16(a, b, dims):
    return lax.dot_general(a, b, dims, preferred_element_type=F32)


def prep_kernel(maps, raw, bias, rate, seg_row, seg_col, payload, run, run_t, step_t):
    num_tok, heads = raw.shape
    dim = maps.shape[1] // 2
    z = raw[...] + bias[...]
    step = jnp.maximum(z, 0.0) + jnp.log1p(jnp.exp(-jnp.abs(z)))
    log_decay = -step * rate[...]
    down = lax.broadcasted_iota(jnp.int32, (num_tok, num_tok), 0)
    along = lax.broadcasted_iota(jnp.int32, (num_tok, num_tok), 1)
    same = seg_row[...] == seg_col[...]
    causal = (same & (down >= along)).astype(F32)
    running = dot32(causal, log_decay, NN)
    totals = dot32(same.astype(F32), log_decay, NN)
    run[...] = running
    run_t[...] = dot32(log_decay, causal, (((0,), (1,)), ((), ())))
    step_t[...] = dot32(step, (down == along).astype(F32), TN)
    weights = jnp.exp(jnp.minimum(totals - running, 0.0)) * step
    grown = jnp.exp(totals)
    high = grown.astype(BF)
    low = (grown - high.astype(F32)).astype(BF)
    payload[:, :dim] = maps[:, dim:].astype(BF)
    payload[:, dim : 2 * dim] = maps[:, :dim].astype(BF)
    head = lax.broadcasted_iota(jnp.int32, (heads, LANES), 0)
    lane = lax.broadcasted_iota(jnp.int32, (heads, LANES), 1)
    tail = jnp.zeros((num_tok, LANES), F32)
    for i, part in enumerate((weights.astype(BF), high, low)):
        tail += dot16(part, (lane == head + i * heads).astype(BF), NN)
    seg_lane = lax.broadcasted_iota(jnp.int32, (num_tok, LANES), 1) == 3 * heads
    tail = jnp.where(seg_lane, seg_row[...].astype(F32), tail)
    payload[:, 2 * dim :] = tail.astype(BF)


def prep(maps, raw, bias, rate, seg):
    num_tok, heads = raw.shape
    return pl.pallas_call(
        prep_kernel,
        out_shape=[
            jax.ShapeDtypeStruct((num_tok, maps.shape[1] + LANES), BF),
            jax.ShapeDtypeStruct((num_tok, heads), F32),
            jax.ShapeDtypeStruct((heads, num_tok), F32),
            jax.ShapeDtypeStruct((heads, num_tok), F32),
        ],
        cost_estimate=pl.CostEstimate(flops=1 << 28, bytes_accessed=1 << 20, transcendentals=1 << 14),
    )(maps, raw, bias[None], rate[None], seg[:, None], seg[None, :])


def carried_kernel(slot, member, payload, *refs):
    *states, out = refs
    heads, width, dim = states[0].shape[1:]
    at = lax.broadcasted_iota(jnp.int32, (1, LANES), 1)
    seg_at = payload.shape[1] - LANES
    tail = payload[:, seg_at:].astype(F32)
    c_part = payload[:, :dim].astype(F32)
    total = jnp.zeros(out.shape, F32)
    seg = jnp.sum(jnp.where(at == member[len(states)], tail, 0.0), axis=1, keepdims=True)
    for rank, state in enumerate(states):
        inside = seg == member[rank].astype(F32)
        mine = jnp.where(inside, c_part, 0.0).astype(BF)
        flat = state[0].reshape(heads * width, dim).astype(BF)
        total += dot16(mine, flat, NT)
    out[...] = total.astype(BF)


def carried_part(slot, member, payload, cache):
    num_tok = payload.shape[0]
    _, heads, width, dim = cache.shape
    chunk = min(heads, 4)
    ranks = slot.shape[0]

    def state_map(rank, i, slot, member):
        return (slot[rank], i, 0, 0)

    return pl.pallas_call(
        carried_kernel,
        out_shape=jax.ShapeDtypeStruct((num_tok, heads * width), BF),
        grid_spec=pltpu.PrefetchScalarGridSpec(
            num_scalar_prefetch=2,
            grid=(heads // chunk,),
            in_specs=[pl.BlockSpec(payload.shape, lambda i, *_: (0, 0))]
            + [
                pl.BlockSpec((1, chunk, width, dim), functools.partial(state_map, rank))
                for rank in range(ranks)
            ],
            out_specs=pl.BlockSpec((num_tok, chunk * width), lambda i, *_: (0, i)),
        ),
        cost_estimate=pl.CostEstimate(
            flops=2 * num_tok * dim * heads * width * ranks,
            bytes_accessed=ranks * heads * width * dim * 4 + num_tok * heads * width * 2,
            transcendentals=0,
        ),
    )(slot, member, payload, *([cache] * ranks))


def within_kernel(owners, *refs):
    parts = refs[:owners]
    payload, seg_row, seg_col, run, run_t, step_t, gain, base, grown, x_t = refs[owners:]
    num_tok, columns = base.shape
    heads = run.shape[1]
    width = columns // heads
    dim = (payload.shape[1] - LANES) // 2
    down = lax.broadcasted_iota(jnp.int32, (num_tok, num_tok), 0)
    along = lax.broadcasted_iota(jnp.int32, (num_tok, num_tok), 1)
    keep = (seg_row[...] == seg_col[...]) & (down >= along)
    raw = dot16(payload[:, :dim], payload[:, dim : 2 * dim], NT)
    scores = jnp.where(keep, raw, 0.0)
    pair = LANES // width
    lane = lax.broadcasted_iota(jnp.int32, (num_tok, LANES), 1) // width
    for first in range(0, heads, pair):
        at = slice(first * width, (first + pair) * width)
        values = parts[0][:, at].astype(F32)
        for part in parts[1:]:
            values += part[:, at].astype(F32)
        values = values.astype(BF)
        exact = values.astype(F32)
        x_t[at, :] = exact.T.astype(BF)
        total = jnp.zeros((num_tok, LANES), F32)
        rise = jnp.zeros((num_tok, LANES), F32)
        for i in range(pair):
            h = first + i
            run_col = run[:, h : h + 1]
            decay = jnp.exp(jnp.minimum(run_col - run_t[h : h + 1, :], 0.0))
            mixing = (decay * scores * step_t[h : h + 1, :]).astype(BF)
            inner = dot16(mixing, values, NN) + gain[:, h : h + 1] * exact
            total = jnp.where(lane == i, inner, total)
            rise = jnp.where(lane == i, jnp.exp(run_col), rise)
        base[:, at] = total
        grown[:, at] = rise


def within_part(parts, payload, seg, run, run_t, step_t, gain):
    num_tok, columns = parts[0].shape
    heads = run.shape[1]
    return pl.pallas_call(
        functools.partial(within_kernel, len(parts)),
        out_shape=[
            jax.ShapeDtypeStruct((num_tok, columns), F32),
            jax.ShapeDtypeStruct((num_tok, columns), F32),
            jax.ShapeDtypeStruct((columns, num_tok), BF),
        ],
        cost_estimate=pl.CostEstimate(
            flops=2 * num_tok * num_tok * columns * 2,
            bytes_accessed=num_tok * columns * (2 * len(parts) + 10),
            transcendentals=num_tok * num_tok * heads,
        ),
    )(*parts, payload, seg[:, None], seg[None, :], run, run_t, step_t, gain[None])


def states_kernel(owners, which, member, state, *refs):
    x_refs, payloads, out = refs[:owners], refs[owners:-1], refs[-1]
    heads, width, dim = state.shape[1:]
    at = pl.program_id(0)

    def update(x_ref, payload):
        tail = payload[:, 2 * dim :].astype(F32).T
        inside = tail[3 * heads : 3 * heads + 1] == member[at].astype(F32)
        weights = jnp.where(inside, tail[:heads], 0.0)
        rise = tail[heads : 2 * heads] + tail[2 * heads : 3 * heads]
        rise = jnp.max(jnp.where(inside, rise, 0.0), axis=1, keepdims=True)
        b_part = payload[:, dim : 2 * dim]
        for h in range(heads):
            rows = slice(h * width, (h + 1) * width)
            scaled = (x_ref[rows, :].astype(F32) * weights[h : h + 1]).astype(BF)
            out[0, h] = state[0, h] * rise[h : h + 1] + dot16(scaled, b_part, NN)

    for i in range(owners):
        pl.when(which[at] == i)(functools.partial(update, x_refs[i], payloads[i]))

    @pl.when(which[at] < 0)
    def _():
        out[...] = state[...]


def states_part(which, member, cache, x_all, payloads):
    slots, heads, width, dim = cache.shape
    columns, num_tok = x_all[0].shape
    slab = pl.BlockSpec((1, heads, width, dim), lambda s, *_: (s, 0, 0, 0))
    return pl.pallas_call(
        functools.partial(states_kernel, len(x_all)),
        out_shape=jax.ShapeDtypeStruct(cache.shape, cache.dtype),
        grid_spec=pltpu.PrefetchScalarGridSpec(
            num_scalar_prefetch=2,
            grid=(slots,),
            in_specs=[slab]
            + [pl.BlockSpec(x.shape, lambda s, *_: (0, 0)) for x in x_all]
            + [pl.BlockSpec(p.shape, lambda s, *_: (0, 0)) for p in payloads],
            out_specs=slab,
        ),
        cost_estimate=pl.CostEstimate(
            flops=2 * slots * num_tok * columns * dim,
            bytes_accessed=cache.size * 8 + len(x_all) * num_tok * columns * 2,
            transcendentals=0,
        ),
    )(which, member, cache, *x_all, *payloads)


def body(
    tokens,
    w_x,
    w_bc,
    w_dt,
    dt_bias,
    decay_rate,
    skip_gain,
    w_out,
    suffix_lengths,
    checkpoint_slot,
    cache,
):
    reqs = lax.axis_size("req")
    tensors = lax.axis_size("tensor")
    chips = tensors // 2
    own_req = lax.axis_index("req")
    own_tensor = lax.axis_index("tensor")
    own_chip = own_tensor // 2
    core = own_tensor % 2
    num_tok = tokens.shape[0]
    depth = w_x.shape[0]
    slots_dev, heads, width, state_dim = cache.shape
    columns = heads * width
    half = depth // 2

    def token_block(req, start, size):
        return lax.dynamic_slice(tokens, (0, req * depth + start), (num_tok, size))

    near = [token_block(own_req, core * half, half)]
    for k in range(1, reqs):
        near.append(turn_req(token_block((own_req + k) % reqs, core * half, half), k))

    share = depth // tensors
    bc_share = lax.dynamic_slice_in_dim(w_bc, own_tensor * share, share)
    small = spread_out(jnp.concatenate([bc_share, w_dt.T.reshape(-1, w_bc.shape[1])], axis=0))
    bc_tokens = lax.dynamic_index_in_dim(
        tokens.reshape(num_tok, reqs, tensors, share), own_tensor, axis=2, keepdims=False
    )
    state_maps = sum_tensor(
        jnp.dot(
            bc_tokens.reshape(num_tok, reqs * share),
            small[:, :share].reshape(reqs * share, -1),
            preferred_element_type=F32,
        )
    )
    raw_step = jnp.einsum(
        "trk,rhk->th",
        tokens.reshape(num_tok, reqs, depth),
        small[:, share:].reshape(reqs, heads, depth),
        preferred_element_type=F32,
    )
    places = jnp.arange(num_tok, dtype=jnp.int32)
    ends = jnp.cumsum(suffix_lengths[0])
    seg = jnp.sum((places[:, None] >= ends[None, :]).astype(jnp.int32), axis=1)
    payload, run, run_t, step_t = prep(state_maps, raw_step, dt_bias, decay_rate, seg)
    payloads = [payload] + [turn_req(payload, k) for k in range(1, reqs)]

    per_pair = (slots_dev + reqs - 1) // reqs
    total_reqs = checkpoint_slot.shape[0]
    req_dev = total_reqs // reqs
    holder = checkpoint_slot // slots_dev
    index = jnp.arange(total_reqs, dtype=jnp.int32)
    owner = index // req_dev
    pair_key = holder * reqs + owner
    rank_in_pair = jnp.sum(
        (pair_key[:, None] == pair_key[None, :])
        & (checkpoint_slot[None, :] < checkpoint_slot[:, None]),
        axis=1,
    )
    away = (own_req - owner) % reqs
    pairs = jnp.arange(reqs * per_pair, dtype=jnp.int32)
    match = (holder == own_req)[None, :] & (
        (away * per_pair + rank_in_pair)[None, :] == pairs[:, None]
    )

    def pick(match, values, missing):
        found = jnp.sum(jnp.where(match, values[None, :], 0), axis=1)
        return jnp.where(jnp.any(match, axis=1), found, missing).astype(jnp.int32)

    pair_slot = pick(match, checkpoint_slot % slots_dev, 0).reshape(reqs, per_pair)
    pair_member = pick(match, index % req_dev, -1).reshape(reqs, per_pair)
    seg_lane = jnp.full((reqs, 1), 3 * heads, jnp.int32)
    pair_member = jnp.concatenate([pair_member, seg_lane], axis=1)

    w_near = lax.dynamic_slice_in_dim(w_x, core * half, half)
    w_far = lax.dynamic_slice_in_dim(w_x, (1 - core) * half, half)
    parts = []
    for k in range(reqs):
        partial = jnp.dot(near[k], w_near, preferred_element_type=F32) + jnp.dot(
            swap_core(near[k]), w_far, preferred_element_type=F32
        )
        parts.append(partial.astype(BF))
    parts = [parts[0]] + [turn_req(parts[k], -k) for k in range(1, reqs)]

    carried = [
        carried_part(pair_slot[k], pair_member[k], payloads[k], cache) for k in range(reqs)
    ]
    carried = [carried[0]] + [turn_req(carried[k], -k) for k in range(1, reqs)]

    base, grown, x_t = within_part(parts, payload, seg, run, run_t, step_t, skip_gain)
    held = carried[0].astype(F32)
    for k in range(1, reqs):
        held = held + carried[k].astype(F32)
    outputs = (base + grown * held).astype(BF)

    rows_half = num_tok // 2
    arrived = []
    for k in range(reqs):
        block = outputs if k == 0 else turn_req(outputs, k)
        product = jnp.dot(block, w_out, preferred_element_type=F32).astype(BF)
        kept = lax.dynamic_slice_in_dim(product, core * rows_half, rows_half)
        given = lax.dynamic_slice_in_dim(product, (1 - core) * rows_half, rows_half)
        summed = (kept.astype(F32) + swap_core(given).astype(F32)).astype(BF)
        arrived.append(summed if k == 0 else turn_req(summed, -k))

    def column_block(req):
        chosen = arrived[0]
        for k in range(1, reqs):
            chosen = jnp.where((req - own_req) % reqs == k, arrived[k], chosen)
        return chosen

    pair_blocks = [
        jnp.stack([column_block(2 * ((own_chip + turn) % chips) + c) for c in range(2)])
        for turn in range(chips)
    ]
    total = pair_blocks[0].astype(F32)
    for turn in range(1, chips):
        total = total + turn_chip(pair_blocks[turn], turn).astype(F32)
    total = total.astype(BF)
    kept = lax.dynamic_index_in_dim(total, core, axis=0, keepdims=False)
    other = swap_core(lax.dynamic_index_in_dim(total, 1 - core, axis=0, keepdims=False))
    layer_out = jnp.concatenate(
        [jnp.where(core == 0, kept, other), jnp.where(core == 0, other, kept)], axis=0
    )

    x_all = [x_t] + [turn_req(x_t, k) for k in range(1, reqs)]
    slot_ids = own_req * slots_dev + jnp.arange(slots_dev, dtype=jnp.int32)
    match_slot = checkpoint_slot[None, :] == slot_ids[:, None]
    new_cache = states_part(
        pick(match_slot, away, -1), pick(match_slot, index % req_dev, -1), cache, x_all, payloads
    )
    return (layer_out, new_cache)


def solution(mesh):
    placed = (
        P(("groups", "req"), None),
        P("req", "tensor"),
        P("req", None),
        P("req", "tensor"),
        P("tensor"),
        P("tensor"),
        P("tensor"),
        P("tensor", "req"),
        P(("groups", "req"), None),
        P("groups"),
        P(("groups", "req"), "tensor", None, None),
    )
    return jax.shard_map(
        body,
        mesh=mesh,
        in_specs=placed,
        out_specs=(P(("groups", "req"), "tensor"), P(("groups", "req"), "tensor", None, None)),
        check_vma=False,
    )
```

```python
import functools

import jax
import jax.numpy as jnp
from jax import lax
from jax.experimental import pallas as pl
from jax.experimental.pallas import tpu as pltpu
from jax.sharding import PartitionSpec as P

HIGH = lax.Precision.HIGHEST
BF = jnp.bfloat16
F32 = jnp.float32
NN = (((1,), (0,)), ((), ()))
NT = (((1,), (1,)), ((), ()))
TN = (((0,), (0,)), ((), ()))
LANES = 128


def turn_req(x, turn):
    count = lax.axis_size("req")
    return lax.ppermute(x, "req", [(i, (i + turn) % count) for i in range(count)])


def step_up(x, first, last):
    return lax.ppermute(x, "req", [(i, i + 1) for i in range(first, last)])


def step_down(x, first, last):
    top = lax.axis_size("req") - 1
    return lax.ppermute(x, "req", [(top - i, top - i - 1) for i in range(first, last)])


def line_gather(x):
    count = lax.axis_size("req")
    below, above = [], []
    low = high = x
    for hop in range(count - 1):
        low, high = step_up(low, hop, count - 1), step_down(high, hop, count - 1)
        below.append(low)
        above.append(high)
    return below, above


def line_sum(blocks):
    count = lax.axis_size("req")
    low, high = blocks[1], blocks[count - 1]
    for hop in range(1, count):
        if hop > 1:
            low, high = low + blocks[hop], high + blocks[count - hop]
        low, high = step_up(low, 0, hop), step_down(high, 0, hop)
    return blocks[0], low, high


def swap_core(x):
    count = lax.axis_size("tensor")
    return lax.ppermute(x, "tensor", [(i, i ^ 1) for i in range(count)])


def turn_chip(x, turn):
    count = lax.axis_size("tensor")
    return lax.ppermute(x, "tensor", [(i, (i + 2 * turn) % count) for i in range(count)])


def spread_out(x):
    count = lax.axis_size("req")
    wide = jnp.broadcast_to(x[None], (count,) + x.shape)
    return lax.all_to_all(wide, "req", split_axis=0, concat_axis=0, tiled=True)


def sum_tensor(x):
    x = x + swap_core(x)
    total = x
    for turn in range(1, lax.axis_size("tensor") // 2):
        total = total + turn_chip(x, turn)
    return total


def dot32(a, b, dims):
    return lax.dot_general(a, b, dims, precision=HIGH, preferred_element_type=F32)


def dot16(a, b, dims):
    return lax.dot_general(a, b, dims, preferred_element_type=F32)


def prep_kernel(maps, raw, bias, rate, seg_row, seg_col, payload, b_part, run, run_t, step_t):
    num_tok, heads = raw.shape
    dim = maps.shape[1] // 2
    z = raw[...] + bias[...]
    step = jnp.maximum(z, 0.0) + jnp.log1p(jnp.exp(-jnp.abs(z)))
    log_decay = -step * rate[...]
    down = lax.broadcasted_iota(jnp.int32, (num_tok, num_tok), 0)
    along = lax.broadcasted_iota(jnp.int32, (num_tok, num_tok), 1)
    same = seg_row[...] == seg_col[...]
    causal = (same & (down >= along)).astype(F32)
    running = dot32(causal, log_decay, NN)
    totals = dot32(same.astype(F32), log_decay, NN)
    run[...] = running
    run_t[...] = dot32(log_decay, causal, (((0,), (1,)), ((), ())))
    step_t[...] = dot32(step, (down == along).astype(F32), TN)
    weights = jnp.exp(jnp.minimum(totals - running, 0.0)) * step
    grown = jnp.exp(totals)
    high = grown.astype(BF)
    low = (grown - high.astype(F32)).astype(BF)
    payload[:, :dim] = maps[:, dim:].astype(BF)
    b_part[...] = maps[:, :dim].astype(BF)
    head = lax.broadcasted_iota(jnp.int32, (heads, LANES), 0)
    lane = lax.broadcasted_iota(jnp.int32, (heads, LANES), 1)
    tail = jnp.zeros((num_tok, LANES), F32)
    for i, part in enumerate((weights.astype(BF), high, low)):
        tail += dot16(part, (lane == head + i * heads).astype(BF), NN)
    seg_lane = lax.broadcasted_iota(jnp.int32, (num_tok, LANES), 1) == 3 * heads
    tail = jnp.where(seg_lane, seg_row[...].astype(F32), tail)
    payload[:, dim:] = tail.astype(BF)


def prep(maps, raw, bias, rate, seg):
    num_tok, heads = raw.shape
    return pl.pallas_call(
        prep_kernel,
        out_shape=[
            jax.ShapeDtypeStruct((num_tok, maps.shape[1] // 2 + LANES), BF),
            jax.ShapeDtypeStruct((num_tok, maps.shape[1] // 2), BF),
            jax.ShapeDtypeStruct((num_tok, heads), F32),
            jax.ShapeDtypeStruct((heads, num_tok), F32),
            jax.ShapeDtypeStruct((heads, num_tok), F32),
        ],
        cost_estimate=pl.CostEstimate(flops=1 << 28, bytes_accessed=1 << 20, transcendentals=1 << 14),
    )(maps, raw, bias[None], rate[None], seg[:, None], seg[None, :])


def carried_kernel(slot, member, payload, *refs):
    *states, out = refs
    heads, width, dim = states[0].shape[1:]
    at = lax.broadcasted_iota(jnp.int32, (1, LANES), 1)
    seg_at = payload.shape[1] - LANES
    tail = payload[:, seg_at:].astype(F32)
    c_part = payload[:, :dim].astype(F32)
    total = jnp.zeros(out.shape, F32)
    seg = jnp.sum(jnp.where(at == member[len(states)], tail, 0.0), axis=1, keepdims=True)
    for rank, state in enumerate(states):
        inside = seg == member[rank].astype(F32)
        mine = jnp.where(inside, c_part, 0.0).astype(BF)
        flat = state[0].reshape(heads * width, dim).astype(BF)
        total += dot16(mine, flat, NT)
    out[...] = total.astype(BF)


def carried_part(slot, member, payload, cache):
    num_tok = payload.shape[0]
    _, heads, width, dim = cache.shape
    ranks = slot.shape[0]

    def state_map(rank, i, slot, member):
        return (slot[rank], 0, 0, 0)

    return pl.pallas_call(
        carried_kernel,
        out_shape=jax.ShapeDtypeStruct((num_tok, heads * width), BF),
        grid_spec=pltpu.PrefetchScalarGridSpec(
            num_scalar_prefetch=2,
            grid=(1,),
            in_specs=[pl.BlockSpec(payload.shape, lambda i, *_: (0, 0))]
            + [
                pl.BlockSpec((1, heads, width, dim), functools.partial(state_map, rank))
                for rank in range(ranks)
            ],
            out_specs=pl.BlockSpec((num_tok, heads * width), lambda i, *_: (0, 0)),
        ),
        cost_estimate=pl.CostEstimate(
            flops=2 * num_tok * dim * heads * width * ranks,
            bytes_accessed=ranks * heads * width * dim * 4 + num_tok * heads * width * 2,
            transcendentals=0,
        ),
    )(slot, member, payload, *([cache] * ranks))


def within_kernel(x, payload, b_part, seg_row, seg_col, run, run_t, step_t, gain, base, grown):
    num_tok, columns = base.shape
    heads = run.shape[1]
    width = columns // heads
    dim = b_part.shape[1]
    down = lax.broadcasted_iota(jnp.int32, (num_tok, num_tok), 0)
    along = lax.broadcasted_iota(jnp.int32, (num_tok, num_tok), 1)
    keep = (seg_row[...] == seg_col[...]) & (down >= along)
    raw = dot16(payload[:, :dim], b_part[...], NT)
    scores = jnp.where(keep, raw, 0.0)
    pair = LANES // width
    lane = lax.broadcasted_iota(jnp.int32, (num_tok, LANES), 1) // width
    for first in range(0, heads, pair):
        at = slice(first * width, (first + pair) * width)
        values = x[:, at]
        exact = values.astype(F32)
        total = jnp.zeros((num_tok, LANES), F32)
        rise = jnp.zeros((num_tok, LANES), F32)
        for i in range(pair):
            h = first + i
            run_col = run[:, h : h + 1]
            decay = jnp.exp(jnp.minimum(run_col - run_t[h : h + 1, :], 0.0))
            mixing = (decay * scores * step_t[h : h + 1, :]).astype(BF)
            inner = dot16(mixing, values, NN) + gain[:, h : h + 1] * exact
            total = jnp.where(lane == i, inner, total)
            rise = jnp.where(lane == i, jnp.exp(run_col), rise)
        base[:, at] = total
        grown[:, at] = rise


def within_part(x, payload, b_part, seg, run, run_t, step_t, gain):
    num_tok, columns = x.shape
    heads = run.shape[1]
    return pl.pallas_call(
        within_kernel,
        out_shape=[jax.ShapeDtypeStruct((num_tok, columns), F32)] * 2,
        cost_estimate=pl.CostEstimate(
            flops=2 * num_tok * num_tok * columns * 2,
            bytes_accessed=num_tok * columns * 10,
            transcendentals=num_tok * num_tok * heads,
        ),
    )(x, payload, b_part, seg[:, None], seg[None, :], run, run_t, step_t, gain[None])


def states_kernel(owners, which, member, state, *refs):
    sources = 2 * owners - 1
    x_refs, refs, out = refs[:sources], refs[sources:-1], refs[-1]
    payloads, b_parts = refs[:owners], refs[owners:]
    heads, width, dim = state.shape[1:]
    at = pl.program_id(0)

    def update(x_ref, payload, b_part):
        tail = payload[:, dim:].astype(F32).T
        inside = tail[3 * heads : 3 * heads + 1] == member[at].astype(F32)
        weights = jnp.where(inside, tail[:heads], 0.0)
        rise = tail[heads : 2 * heads] + tail[2 * heads : 3 * heads]
        rise = jnp.max(jnp.where(inside, rise, 0.0), axis=1, keepdims=True)
        for h in range(heads):
            rows = slice(h * width, (h + 1) * width)
            scaled = (x_ref[rows, :].astype(F32) * weights[h : h + 1]).astype(BF)
            out[0, h] = state[0, h] * rise[h : h + 1] + dot16(scaled, b_part[...], NN)

    for i in range(sources):
        away = i if i < owners else 2 * owners - 1 - i
        pl.when(which[at] == i)(
            functools.partial(update, x_refs[i], payloads[away], b_parts[away])
        )

    @pl.when(which[at] < 0)
    def _():
        out[...] = state[...]


def states_part(which, member, cache, x_all, payloads, b_parts):
    slots, heads, width, dim = cache.shape
    columns, num_tok = x_all[0].shape
    slab = pl.BlockSpec((1, heads, width, dim), lambda s, *_: (s, 0, 0, 0))
    fixed = [*x_all, *payloads, *b_parts]
    return pl.pallas_call(
        functools.partial(states_kernel, len(payloads)),
        out_shape=jax.ShapeDtypeStruct(cache.shape, cache.dtype),
        grid_spec=pltpu.PrefetchScalarGridSpec(
            num_scalar_prefetch=2,
            grid=(slots,),
            in_specs=[slab] + [pl.BlockSpec(x.shape, lambda s, *_: (0, 0)) for x in fixed],
            out_specs=slab,
        ),
        cost_estimate=pl.CostEstimate(
            flops=2 * slots * num_tok * columns * dim,
            bytes_accessed=cache.size * 8 + len(x_all) * num_tok * columns * 2,
            transcendentals=0,
        ),
    )(which, member, cache, *fixed)


def body(
    tokens,
    w_x,
    w_bc,
    w_dt,
    dt_bias,
    decay_rate,
    skip_gain,
    w_out,
    suffix_lengths,
    checkpoint_slot,
    cache,
):
    reqs = lax.axis_size("req")
    tensors = lax.axis_size("tensor")
    chips = tensors // 2
    own_req = lax.axis_index("req")
    own_tensor = lax.axis_index("tensor")
    own_chip = own_tensor // 2
    core = own_tensor % 2
    num_tok = tokens.shape[0]
    depth = w_x.shape[0]
    slots_dev, heads, width, state_dim = cache.shape
    columns = heads * width
    half = depth // 2
    piece = num_tok // chips

    def chip_rows(x, place):
        return lax.dynamic_slice_in_dim(x, ((own_chip - place) % chips) * piece, piece)

    near = []
    for k in range(1, reqs):
        start = ((own_req + k) % reqs) * depth + core * half
        block = lax.dynamic_slice(tokens, (own_chip * piece, start), (piece, half))
        block = turn_req(block, k)
        pieces = [block] + [turn_chip(block, turn) for turn in range(1, chips)]
        near.append(jnp.concatenate(pieces, axis=0))

    share = depth // tensors
    bc_share = lax.dynamic_slice_in_dim(w_bc, own_tensor * share, share)
    small = spread_out(jnp.concatenate([bc_share, w_dt.T.reshape(-1, w_bc.shape[1])], axis=0))
    bc_tokens = lax.dynamic_index_in_dim(
        tokens.reshape(num_tok, reqs, tensors, share), own_tensor, axis=2, keepdims=False
    )
    state_maps = sum_tensor(
        jnp.dot(
            bc_tokens.reshape(num_tok, reqs * share),
            small[:, :share].reshape(reqs * share, -1),
            preferred_element_type=F32,
        )
    )
    raw_step = jnp.einsum(
        "trk,rhk->th",
        tokens.reshape(num_tok, reqs, depth),
        small[:, share:].reshape(reqs, heads, depth),
        preferred_element_type=F32,
    )
    places = jnp.arange(num_tok, dtype=jnp.int32)
    ends = jnp.cumsum(suffix_lengths[0])
    seg = jnp.sum((places[:, None] >= ends[None, :]).astype(jnp.int32), axis=1)
    payload, b_part, run, run_t, step_t = prep(state_maps, raw_step, dt_bias, decay_rate, seg)
    payloads = [payload] + [turn_req(payload, k) for k in range(1, reqs)]
    b_parts = [b_part] + [turn_req(b_part, k) for k in range(1, reqs)]

    per_pair = (slots_dev + reqs - 1) // reqs
    total_reqs = checkpoint_slot.shape[0]
    req_dev = total_reqs // reqs
    holder = checkpoint_slot // slots_dev
    index = jnp.arange(total_reqs, dtype=jnp.int32)
    owner = index // req_dev
    pair_key = holder * reqs + owner
    rank_in_pair = jnp.sum(
        (pair_key[:, None] == pair_key[None, :])
        & (checkpoint_slot[None, :] < checkpoint_slot[:, None]),
        axis=1,
    )
    away = (own_req - owner) % reqs
    pairs = jnp.arange(reqs * per_pair, dtype=jnp.int32)
    match = (holder == own_req)[None, :] & (
        (away * per_pair + rank_in_pair)[None, :] == pairs[:, None]
    )

    def pick(match, values, missing):
        found = jnp.sum(jnp.where(match, values[None, :], 0), axis=1)
        return jnp.where(jnp.any(match, axis=1), found, missing).astype(jnp.int32)

    pair_slot = pick(match, checkpoint_slot % slots_dev, 0).reshape(reqs, per_pair)
    pair_member = pick(match, index % req_dev, -1).reshape(reqs, per_pair)
    seg_lane = jnp.full((reqs, 1), 3 * heads, jnp.int32)
    pair_member = jnp.concatenate([pair_member, seg_lane], axis=1)

    w_near = lax.dynamic_slice_in_dim(w_x, core * half, half)
    w_far = lax.dynamic_slice_in_dim(w_x, (1 - core) * half, half)
    own_block = lax.dynamic_slice(tokens, (0, own_req * depth), (num_tok, depth))
    own_block = jnp.concatenate([chip_rows(own_block, place) for place in range(chips)], axis=0)
    total = jnp.dot(own_block, w_x, preferred_element_type=F32)
    for k in range(1, reqs):
        partial = jnp.dot(near[k - 1], w_near, preferred_element_type=F32) + jnp.dot(
            swap_core(near[k - 1]), w_far, preferred_element_type=F32
        )
        total = total + turn_req(partial.astype(BF), -k).astype(F32)
    values = total.astype(BF)
    values = jnp.concatenate([chip_rows(values, place) for place in range(chips)], axis=0)

    carried = line_sum(
        [carried_part(pair_slot[k], pair_member[k], payloads[k], cache) for k in range(reqs)]
    )

    base, grown = within_part(values, payload, b_part, seg, run, run_t, step_t, skip_gain)
    held = sum(block.astype(F32) for block in carried)
    outputs = (base + grown * held).astype(BF)

    rows_half = num_tok // 2

    def project(block):
        product = jnp.dot(block, w_out, preferred_element_type=F32).astype(BF)
        kept = lax.dynamic_slice_in_dim(product, core * rows_half, rows_half)
        given = lax.dynamic_slice_in_dim(product, (1 - core) * rows_half, rows_half)
        return (kept.astype(F32) + swap_core(given).astype(F32)).astype(BF)

    below, above = line_gather(outputs)
    arrived = [project(outputs)]
    from_above, from_below = [], []
    for k in range(1, reqs):
        down = [(i, i - k) for i in range(k, reqs)]
        up = [(i, i + k) for i in range(reqs - k)]
        from_above.append(lax.ppermute(project(below[k - 1]), "req", down))
        from_below.append(lax.ppermute(project(above[k - 1]), "req", up))
    arrived += [from_above[k] + from_below[reqs - 2 - k] for k in range(reqs - 1)]

    def column_block(req):
        chosen = arrived[0]
        for k in range(1, reqs):
            chosen = jnp.where((req - own_req) % reqs == k, arrived[k], chosen)
        return chosen

    pair_blocks = [
        jnp.stack([column_block(2 * ((own_chip + turn) % chips) + c) for c in range(2)])
        for turn in range(chips)
    ]
    total = pair_blocks[0].astype(F32)
    for turn in range(1, chips):
        total = total + turn_chip(pair_blocks[turn], turn).astype(F32)
    total = total.astype(BF)
    kept = lax.dynamic_index_in_dim(total, core, axis=0, keepdims=False)
    other = swap_core(lax.dynamic_index_in_dim(total, 1 - core, axis=0, keepdims=False))
    layer_out = jnp.concatenate(
        [jnp.where(core == 0, kept, other), jnp.where(core == 0, other, kept)], axis=0
    )

    x_t = values.T
    x_below, x_above = line_gather(x_t)
    which = jnp.where(owner <= own_req, own_req - owner, reqs - 1 + owner - own_req)
    slot_ids = own_req * slots_dev + jnp.arange(slots_dev, dtype=jnp.int32)
    match_slot = checkpoint_slot[None, :] == slot_ids[:, None]
    new_cache = states_part(
        pick(match_slot, which, -1),
        pick(match_slot, index % req_dev, -1),
        cache,
        [x_t, *x_below, *x_above],
        payloads,
        b_parts,
    )
    return (layer_out, new_cache)


def solution(mesh):
    placed = (
        P(("groups", "req"), None),
        P("req", "tensor"),
        P("req", None),
        P("req", "tensor"),
        P("tensor"),
        P("tensor"),
        P("tensor"),
        P("tensor", "req"),
        P(("groups", "req"), None),
        P("groups"),
        P(("groups", "req"), "tensor", None, None),
    )
    return jax.shard_map(
        body,
        mesh=mesh,
        in_specs=placed,
        out_specs=(P(("groups", "req"), "tensor"), P(("groups", "req"), "tensor", None, None)),
        check_vma=False,
    )
```

```python
import functools

import jax
import jax.numpy as jnp
from jax import lax
from jax.experimental import pallas as pl
from jax.experimental.pallas import tpu as pltpu
from jax.sharding import PartitionSpec as P

HIGH = lax.Precision.HIGHEST
BF = jnp.bfloat16
F32 = jnp.float32
NN = (((1,), (0,)), ((), ()))
NT = (((1,), (1,)), ((), ()))
TN = (((0,), (0,)), ((), ()))
TT = (((0,), (1,)), ((), ()))
LANES = 128


def turn_req(x, turn):
    count = lax.axis_size("req")
    return lax.ppermute(x, "req", [(i, (i + turn) % count) for i in range(count)])


def swap_core(x):
    count = lax.axis_size("tensor")
    return lax.ppermute(x, "tensor", [(i, i ^ 1) for i in range(count)])


def turn_chip(x, turn):
    count = lax.axis_size("tensor")
    return lax.ppermute(x, "tensor", [(i, (i + 2 * turn) % count) for i in range(count)])


def spread_out(x):
    count = lax.axis_size("req")
    wide = jnp.broadcast_to(x[None], (count,) + x.shape)
    return lax.all_to_all(wide, "req", split_axis=0, concat_axis=0, tiled=True)


def sum_tensor(x):
    x = x + swap_core(x)
    total = x
    for turn in range(1, lax.axis_size("tensor") // 2):
        total = total + turn_chip(x, turn)
    return total


def dot32(a, b, dims):
    return lax.dot_general(a, b, dims, precision=HIGH, preferred_element_type=F32)


def dot16(a, b, dims):
    return lax.dot_general(a, b, dims, preferred_element_type=F32)


def prep_kernel(maps, raw, bias, rate, seg_row, seg_col, c_seg, tail_t, c_part, b_part, run, run_t, step_t):
    num_tok, heads = raw.shape
    dim = maps.shape[1] // 2
    z = raw[...] + bias[...]
    step = jnp.maximum(z, 0.0) + jnp.log1p(jnp.exp(-jnp.abs(z)))
    log_decay = -step * rate[...]
    down = lax.broadcasted_iota(jnp.int32, (num_tok, num_tok), 0)
    along = lax.broadcasted_iota(jnp.int32, (num_tok, num_tok), 1)
    same = seg_row[...] == seg_col[...]
    causal = (same & (down >= along)).astype(F32)
    run[...] = dot32(causal, log_decay, NN)
    flat_t = dot32(log_decay, causal, TT)
    run_t[...] = flat_t
    totals_t = dot32(log_decay, same.astype(F32), TN)
    flat_step = dot32(step, (down == along).astype(F32), TN)
    step_t[...] = flat_step
    grown = jnp.exp(totals_t)
    high = grown.astype(BF)
    tail_t[...] = jnp.zeros_like(tail_t)
    tail_t[:heads, :] = (jnp.exp(jnp.minimum(totals_t - flat_t, 0.0)) * flat_step).astype(BF)
    tail_t[16 : 16 + heads, :] = high
    tail_t[32 : 32 + heads, :] = (grown - high.astype(F32)).astype(BF)
    seg_rows = jnp.broadcast_to(seg_col[...].astype(F32), (16, num_tok)).astype(BF)
    tail_t[48:64, :] = seg_rows
    c_seg[:dim, :] = maps[:, dim:].T.astype(BF)
    c_seg[dim:, :] = seg_rows
    c_part[...] = maps[:, dim:].astype(BF)
    b_part[...] = maps[:, :dim].astype(BF)


def prep(maps, raw, bias, rate, seg):
    num_tok, heads = raw.shape
    dim = maps.shape[1] // 2
    return pl.pallas_call(
        prep_kernel,
        out_shape=[
            jax.ShapeDtypeStruct((dim + 16, num_tok), BF),
            jax.ShapeDtypeStruct((64, num_tok), BF),
            jax.ShapeDtypeStruct((num_tok, dim), BF),
            jax.ShapeDtypeStruct((num_tok, dim), BF),
            jax.ShapeDtypeStruct((num_tok, heads), F32),
            jax.ShapeDtypeStruct((heads, num_tok), F32),
            jax.ShapeDtypeStruct((heads, num_tok), F32),
        ],
        cost_estimate=pl.CostEstimate(flops=1 << 28, bytes_accessed=1 << 20, transcendentals=1 << 14),
    )(maps, raw, bias[None], rate[None], seg[:, None], seg[None, :])


def carried_kernel(owners, slot, member, *refs):
    c_segs, states, outs = refs[:owners], refs[owners:-owners], refs[-owners:]
    heads, width, dim = states[0].shape[1:]
    at = pl.program_id(0)
    ranks = len(states)
    flat = [state[0].reshape(heads * width, dim).astype(BF) for state in states]

    def fill(c_seg, out):
        c_rows = c_seg[:dim, :].astype(F32)
        seg = c_seg[dim : dim + 1, :].astype(F32)
        total = jnp.zeros(out.shape, F32)
        for rank in range(ranks):
            inside = seg == member[at * ranks + rank].astype(F32)
            mine = jnp.where(inside, c_rows, 0.0).T.astype(BF)
            total += dot16(mine, flat[rank], NT)
        out[...] = total.astype(BF)

    for i in range(owners):
        pl.when(at == i)(functools.partial(fill, c_segs[i], outs[i]))


def carried_part(slot, member, c_segs, cache):
    num_tok = c_segs[0].shape[1]
    _, heads, width, dim = cache.shape
    owners = len(c_segs)
    ranks = slot.shape[0] // owners

    def state_map(rank, i, slot, member):
        return (slot[i * ranks + rank], 0, 0, 0)

    return pl.pallas_call(
        functools.partial(carried_kernel, owners),
        out_shape=[jax.ShapeDtypeStruct((num_tok, heads * width), BF)] * owners,
        grid_spec=pltpu.PrefetchScalarGridSpec(
            num_scalar_prefetch=2,
            grid=(owners,),
            in_specs=[pl.BlockSpec(c_seg.shape, lambda i, *_: (0, 0)) for c_seg in c_segs]
            + [
                pl.BlockSpec((1, heads, width, dim), functools.partial(state_map, rank))
                for rank in range(ranks)
            ],
            out_specs=[pl.BlockSpec((num_tok, heads * width), lambda i, *_: (0, 0))] * owners,
        ),
        cost_estimate=pl.CostEstimate(
            flops=2 * owners * num_tok * dim * heads * width * ranks,
            bytes_accessed=owners * (ranks * dim * 4 + num_tok * 2) * heads * width,
            transcendentals=0,
        ),
    )(slot, member, *c_segs, *([cache] * ranks))


def gather_kernel(count, chips, chip, *refs):
    parts = refs[:count]
    b_part, tail_t, x, bundle = refs[count:]
    num_tok, columns = x.shape
    dim = b_part.shape[1]
    piece = num_tok // chips
    for place in range(chips):
        rows = pl.ds(pl.multiple_of(lax.rem(chip[0] - place + chips, chips) * piece, piece), piece)
        at = slice(place * piece, (place + 1) * piece)
        total = parts[0][at, :].astype(F32)
        for part in parts[1:]:
            total += part[at, :].astype(F32)
        x[rows, :] = total.astype(BF)
    for first in range(0, columns, LANES):
        at = slice(first, first + LANES)
        bundle[at, :] = x[:, at].astype(F32).T.astype(BF)
    bundle[columns : columns + dim, :] = b_part[...].astype(F32).T.astype(BF)
    bundle[columns + dim :, :] = tail_t[...]


def gather_part(parts, b_part, tail_t, chip, chips):
    num_tok, columns = parts[0].shape
    rows = columns + b_part.shape[1] + tail_t.shape[0]
    vmem = pl.BlockSpec(memory_space=pltpu.VMEM)
    return pl.pallas_call(
        functools.partial(gather_kernel, len(parts), chips),
        out_shape=[
            jax.ShapeDtypeStruct((num_tok, columns), BF),
            jax.ShapeDtypeStruct((rows, num_tok), BF),
        ],
        in_specs=[pl.BlockSpec(memory_space=pltpu.SMEM)] + [vmem] * (len(parts) + 2),
        cost_estimate=pl.CostEstimate(
            flops=num_tok * columns * len(parts),
            bytes_accessed=num_tok * columns * 2 * (len(parts) + 2),
            transcendentals=0,
        ),
    )(chip.reshape(1).astype(jnp.int32), *parts, b_part, tail_t)


def within_kernel(x, c_part, b_part, seg_row, seg_col, run, run_t, step_t, gain, base, grown):
    num_tok, columns = base.shape
    heads = run.shape[1]
    width = columns // heads
    down = lax.broadcasted_iota(jnp.int32, (num_tok, num_tok), 0)
    along = lax.broadcasted_iota(jnp.int32, (num_tok, num_tok), 1)
    keep = (seg_row[...] == seg_col[...]) & (down >= along)
    raw = dot16(c_part[...], b_part[...], NT)
    scores = jnp.where(keep, raw, 0.0)
    pair = LANES // width
    lane = lax.broadcasted_iota(jnp.int32, (num_tok, LANES), 1) // width
    for first in range(0, heads, pair):
        at = slice(first * width, (first + pair) * width)
        values = x[:, at]
        exact = values.astype(F32)
        total = jnp.zeros((num_tok, LANES), F32)
        rise = jnp.zeros((num_tok, LANES), F32)
        for i in range(pair):
            h = first + i
            run_col = run[:, h : h + 1]
            decay = jnp.exp(jnp.minimum(run_col - run_t[h : h + 1, :], 0.0))
            mixing = (decay * scores * step_t[h : h + 1, :]).astype(BF)
            inner = dot16(mixing, values, NN) + gain[:, h : h + 1] * exact
            total = jnp.where(lane == i, inner, total)
            rise = jnp.where(lane == i, jnp.exp(run_col), rise)
        base[:, at] = total
        grown[:, at] = rise


def within_part(x, c_part, b_part, seg, run, run_t, step_t, gain):
    num_tok, columns = x.shape
    heads = run.shape[1]
    return pl.pallas_call(
        within_kernel,
        out_shape=[jax.ShapeDtypeStruct((num_tok, columns), F32)] * 2,
        cost_estimate=pl.CostEstimate(
            flops=2 * num_tok * num_tok * columns * 2,
            bytes_accessed=num_tok * columns * 10,
            transcendentals=num_tok * num_tok * heads,
        ),
    )(x, c_part, b_part, seg[:, None], seg[None, :], run, run_t, step_t, gain[None])


def states_kernel(owner, member, state, bundle, out):
    heads, width, dim = state.shape[1:]
    columns = heads * width
    at = pl.program_id(0)

    @pl.when(member[at] >= 0)
    def _():
        b_rows = bundle[0, columns : columns + dim, :]
        tail = bundle[0, columns + dim :, :].astype(F32)
        inside = tail[48:49] == member[at].astype(F32)
        weights = jnp.where(inside, tail[:heads], 0.0)
        rise = tail[16 : 16 + heads] + tail[32 : 32 + heads]
        rise = jnp.max(jnp.where(inside, rise, 0.0), axis=1, keepdims=True)
        for h in range(heads):
            rows = slice(h * width, (h + 1) * width)
            scaled = (bundle[0, rows, :].astype(F32) * weights[h : h + 1]).astype(BF)
            out[0, h] = state[0, h] * rise[h : h + 1] + dot16(scaled, b_rows, NT)

    @pl.when(member[at] < 0)
    def _():
        out[...] = state[...]


def states_part(owner, member, cache, bundles):
    slots, heads, width, dim = cache.shape
    _, rows, num_tok = bundles.shape
    slab = pl.BlockSpec((1, heads, width, dim), lambda s, *_: (s, 0, 0, 0))
    return pl.pallas_call(
        states_kernel,
        out_shape=jax.ShapeDtypeStruct(cache.shape, cache.dtype),
        grid_spec=pltpu.PrefetchScalarGridSpec(
            num_scalar_prefetch=2,
            grid=(slots,),
            in_specs=[
                slab,
                pl.BlockSpec((1, rows, num_tok), lambda s, owner, member: (owner[s], 0, 0)),
            ],
            out_specs=slab,
        ),
        cost_estimate=pl.CostEstimate(
            flops=2 * slots * num_tok * heads * width * dim,
            bytes_accessed=cache.size * 8 + slots * rows * num_tok * 2,
            transcendentals=0,
        ),
    )(owner, member, cache, bundles)


def body(
    tokens,
    w_x,
    w_bc,
    w_dt,
    dt_bias,
    decay_rate,
    skip_gain,
    w_out,
    suffix_lengths,
    checkpoint_slot,
    cache,
):
    reqs = lax.axis_size("req")
    tensors = lax.axis_size("tensor")
    chips = tensors // 2
    own_req = lax.axis_index("req")
    own_tensor = lax.axis_index("tensor")
    own_chip = own_tensor // 2
    core = own_tensor % 2
    num_tok = tokens.shape[0]
    depth = w_x.shape[0]
    slots_dev, heads, width, state_dim = cache.shape
    columns = heads * width
    half = depth // 2
    piece = num_tok // chips
    piece = num_tok // chips

    share = depth // tensors
    bc_share = lax.dynamic_slice_in_dim(w_bc, own_tensor * share, share)
    small = spread_out(jnp.concatenate([bc_share, w_dt.T.reshape(-1, w_bc.shape[1])], axis=0))
    bc_tokens = lax.dynamic_index_in_dim(
        tokens.reshape(num_tok, reqs, tensors, share), own_tensor, axis=2, keepdims=False
    )
    state_maps = sum_tensor(
        jnp.dot(
            bc_tokens.reshape(num_tok, reqs * share),
            small[:, :share].reshape(reqs * share, -1),
            preferred_element_type=F32,
        )
    )
    raw_step = jnp.einsum(
        "trk,rhk->th",
        tokens.reshape(num_tok, reqs, depth),
        small[:, share:].reshape(reqs, heads, depth),
        preferred_element_type=F32,
    )
    places = jnp.arange(num_tok, dtype=jnp.int32)
    ends = jnp.cumsum(suffix_lengths[0])
    seg = jnp.sum((places[:, None] >= ends[None, :]).astype(jnp.int32), axis=1)
    c_seg, tail_t, c_part, b_part, run, run_t, step_t = prep(
        state_maps, raw_step, dt_bias, decay_rate, seg
    )
    c_segs = [c_seg] + [turn_req(c_seg, k) for k in range(1, reqs)]

    per_pair = (slots_dev + reqs - 1) // reqs
    total_reqs = checkpoint_slot.shape[0]
    req_dev = total_reqs // reqs
    holder = checkpoint_slot // slots_dev
    index = jnp.arange(total_reqs, dtype=jnp.int32)
    owner = index // req_dev
    pair_key = holder * reqs + owner
    rank_in_pair = jnp.sum(
        (pair_key[:, None] == pair_key[None, :])
        & (checkpoint_slot[None, :] < checkpoint_slot[:, None]),
        axis=1,
    )
    away = (own_req - owner) % reqs
    pairs = jnp.arange(reqs * per_pair, dtype=jnp.int32)
    match = (holder == own_req)[None, :] & (
        (away * per_pair + rank_in_pair)[None, :] == pairs[:, None]
    )

    def pick(match, values, missing):
        found = jnp.sum(jnp.where(match, values[None, :], 0), axis=1)
        return jnp.where(jnp.any(match, axis=1), found, missing).astype(jnp.int32)

    pair_slot = pick(match, checkpoint_slot % slots_dev, 0)
    pair_member = pick(match, index % req_dev, -1)

    def chip_rows(x, place):
        return lax.dynamic_slice_in_dim(x, ((own_chip - place) % chips) * piece, piece)

    own_block = lax.dynamic_slice(tokens, (0, own_req * depth), (num_tok, depth))
    own_block = jnp.concatenate([chip_rows(own_block, place) for place in range(chips)], axis=0)
    parts = [jnp.dot(own_block, w_x, preferred_element_type=F32).astype(BF)]
    w_near = lax.dynamic_slice_in_dim(w_x, core * half, half)
    w_far = lax.dynamic_slice_in_dim(w_x, (1 - core) * half, half)
    w_turned = jnp.concatenate([w_near, w_far], axis=0)
    for k in range(1, reqs):
        start = ((own_req + k) % reqs) * depth + core * half
        block = lax.dynamic_slice(tokens, (own_chip * piece, start), (piece, half))
        block = turn_req(block, k)
        pieces = [block] + [turn_chip(block, turn) for turn in range(1, chips)]
        near = jnp.concatenate(pieces, axis=0)
        both = jnp.concatenate([near, swap_core(near)], axis=1)
        partial = jnp.dot(both, w_turned, preferred_element_type=F32).astype(BF)
        parts.append(turn_req(partial, -k))
    x, bundle = gather_part(parts, b_part, tail_t, own_chip, chips)
    bundles = lax.all_gather(bundle, "req", axis=0)

    carried = carried_part(pair_slot, pair_member, c_segs, cache)
    carried = [carried[0]] + [turn_req(carried[k], -k) for k in range(1, reqs)]

    base, grown = within_part(x, c_part, b_part, seg, run, run_t, step_t, skip_gain)
    held = sum(block.astype(F32) for block in carried)
    outputs = (base + grown * held).astype(BF)

    rows_half = num_tok // 2
    rows_share = rows_half // chips

    def project(block):
        product = jnp.dot(block, w_out, preferred_element_type=F32).astype(BF)
        kept = lax.dynamic_slice_in_dim(product, core * rows_half, rows_half)
        given = lax.dynamic_slice_in_dim(product, (1 - core) * rows_half, rows_half)
        summed = (kept.astype(F32) + swap_core(given).astype(F32)).astype(BF)
        total = lax.dynamic_slice_in_dim(summed, own_chip * rows_share, rows_share).astype(F32)
        for turn in range(1, chips):
            to_chip = (own_chip + turn) % chips
            given = lax.dynamic_slice_in_dim(summed, to_chip * rows_share, rows_share)
            total = total + turn_chip(given, turn).astype(F32)
        return total.astype(BF)

    arrived = [project(outputs)]
    for k in range(1, reqs):
        arrived.append(turn_req(project(turn_req(outputs, k)), -k))

    def column_blocks(chip):
        def one(req):
            chosen = arrived[0]
            for k in range(1, reqs):
                chosen = jnp.where((req - own_req) % reqs == k, arrived[k], chosen)
            return chosen

        return jnp.stack([one(2 * chip + c) for c in range(2)])

    shares = [column_blocks(own_chip)]
    for turn in range(1, chips):
        shares.append(turn_chip(column_blocks((own_chip + turn) % chips), turn))
    ordered = []
    for chip in range(chips):
        chosen = shares[0]
        for turn in range(1, chips):
            chosen = jnp.where((own_chip - chip) % chips == turn, shares[turn], chosen)
        ordered.append(chosen)
    ordered = jnp.concatenate(ordered, axis=1)
    kept = lax.dynamic_index_in_dim(ordered, core, axis=0, keepdims=False)
    other = swap_core(lax.dynamic_index_in_dim(ordered, 1 - core, axis=0, keepdims=False))
    layer_out = jnp.concatenate(
        [jnp.where(core == 0, kept, other), jnp.where(core == 0, other, kept)], axis=0
    )

    slot_ids = own_req * slots_dev + jnp.arange(slots_dev, dtype=jnp.int32)
    match_slot = checkpoint_slot[None, :] == slot_ids[:, None]
    new_cache = states_part(
        pick(match_slot, owner, 0), pick(match_slot, index % req_dev, -1), cache, bundles
    )
    return (layer_out, new_cache)


def solution(mesh):
    placed = (
        P(("groups", "req"), None),
        P("req", "tensor"),
        P("req", None),
        P("req", "tensor"),
        P("tensor"),
        P("tensor"),
        P("tensor"),
        P("tensor", "req"),
        P(("groups", "req"), None),
        P("groups"),
        P(("groups", "req"), "tensor", None, None),
    )
    return jax.shard_map(
        body,
        mesh=mesh,
        in_specs=placed,
        out_specs=(P(("groups", "req"), "tensor"), P(("groups", "req"), "tensor", None, None)),
        check_vma=False,
    )
```

```python
import functools

import jax
import jax.numpy as jnp
from jax import lax
from jax.experimental import pallas as pl
from jax.experimental.pallas import tpu as pltpu
from jax.sharding import PartitionSpec as P

HIGH = lax.Precision.HIGHEST
BF = jnp.bfloat16
F32 = jnp.float32
NN = (((1,), (0,)), ((), ()))
NT = (((1,), (1,)), ((), ()))
TN = (((0,), (0,)), ((), ()))
TT = (((0,), (1,)), ((), ()))
LANES = 128
PARAMS = pltpu.CompilerParams(vmem_limit_bytes=24 * 1024 * 1024)
COST = pl.CostEstimate(flops=1, bytes_accessed=1, transcendentals=0)


def turn_req(x, turn):
    count = lax.axis_size("req")
    return lax.ppermute(x, "req", [(i, (i + turn) % count) for i in range(count)])


def step_up(x, first, last):
    return lax.ppermute(x, "req", [(i, i + 1) for i in range(first, last)])


def step_down(x, first, last):
    top = lax.axis_size("req") - 1
    return lax.ppermute(x, "req", [(top - i, top - i - 1) for i in range(first, last)])


def line_gather(x):
    count = lax.axis_size("req")
    below, above = [], []
    low = high = x
    for hop in range(count - 1):
        low, high = step_up(low, hop, count - 1), step_down(high, hop, count - 1)
        below.append(low)
        above.append(high)
    return below, above


def line_sum(blocks):
    count = lax.axis_size("req")
    low, high = blocks[1], blocks[count - 1]
    for hop in range(1, count):
        if hop > 1:
            low, high = low + blocks[hop], high + blocks[count - hop]
        low, high = step_up(low, 0, hop), step_down(high, 0, hop)
    return blocks[0], low, high


def swap_core(x):
    count = lax.axis_size("tensor")
    return lax.ppermute(x, "tensor", [(i, i ^ 1) for i in range(count)])


def turn_chip(x, turn):
    count = lax.axis_size("tensor")
    return lax.ppermute(x, "tensor", [(i, (i + 2 * turn) % count) for i in range(count)])


def turn_tensor(x, turn):
    count = lax.axis_size("tensor")
    return lax.ppermute(x, "tensor", [(i, (i + turn) % count) for i in range(count)])


def dot32(a, b, dims):
    return lax.dot_general(a, b, dims, precision=HIGH, preferred_element_type=F32)


def dot16(a, b, dims):
    return lax.dot_general(a, b, dims, preferred_element_type=F32)


def block_kernel(chips, place, w_small, *refs):
    near, far, (block, small) = refs[:chips], refs[chips:-2], refs[-2:]
    piece, half = near[0].shape

    def fill(core):
        own, other = slice(core * half, (core + 1) * half), slice((1 - core) * half, (2 - core) * half)
        for i in range(chips):
            at = lax.rem(place[0] - i + chips, chips) * piece
            rows = pl.ds(pl.multiple_of(at, piece), piece)
            block[rows, own] = near[i][...]
            block[rows, other] = far[i][...]

    for core in range(2):
        pl.when(place[1] == core)(functools.partial(fill, core))
    sums = dot16(block[...], w_small[...], NN)
    lane = lax.broadcasted_iota(jnp.int32, sums.shape, 1)
    low = (lane >= place[2]) & (lane < place[3])
    high = sums.astype(BF)
    small[...] = jnp.where(low, sums - high.astype(F32), sums).astype(BF)


def block_part(place, w_small, near, far):
    chips = len(near)
    num_tok = near[0].shape[0] * chips
    vmem = pl.BlockSpec(memory_space=pltpu.VMEM)
    return pl.pallas_call(
        functools.partial(block_kernel, chips),
        out_shape=[
            jax.ShapeDtypeStruct((num_tok, w_small.shape[0]), BF),
            jax.ShapeDtypeStruct((num_tok, LANES), BF),
        ],
        in_specs=[pl.BlockSpec(memory_space=pltpu.SMEM)] + [vmem] * (1 + 2 * chips),
        compiler_params=PARAMS,
        cost_estimate=COST,
    )(place, w_small, *near, *far)


def product_kernel(block, weights, *refs):
    refs[-1][...] = dot16(block[...], weights[...], NN).astype(BF)


def product_part(block, weights, before):
    vmem = pl.BlockSpec(memory_space=pltpu.VMEM)
    return pl.pallas_call(
        product_kernel,
        out_shape=jax.ShapeDtypeStruct((block.shape[0], weights.shape[1]), BF),
        in_specs=[vmem, vmem] + [pl.BlockSpec(memory_space=pl.ANY)] * len(before),
        compiler_params=PARAMS,
        cost_estimate=COST,
    )(block, weights, *before)


def fold_kernel(share, heads, count, own, *refs):
    parts, (bc_t, raw_t) = refs[:count], refs[-2:]
    lane = lax.broadcasted_iota(jnp.int32, own.shape, 1)
    total = jnp.where(lane < share + heads, own[...], 0.0)
    for part in parts:
        total += part[...].astype(F32)
    total = total.T
    bc_t[...] = total[:share].astype(BF)
    raw_t[...] = total[share : share + heads] + total[share + heads : share + 2 * heads]


def fold_part(own, parts, share, heads, before):
    num_tok = own.shape[0]
    vmem = pl.BlockSpec(memory_space=pltpu.VMEM)
    rest = pl.BlockSpec(memory_space=pl.ANY)
    return pl.pallas_call(
        functools.partial(fold_kernel, share, heads, len(parts)),
        out_shape=[
            jax.ShapeDtypeStruct((share, num_tok), BF),
            jax.ShapeDtypeStruct((heads, num_tok), F32),
        ],
        in_specs=[vmem] * (1 + len(parts)) + [rest] * len(before),
        compiler_params=PARAMS,
        cost_estimate=COST,
    )(own, *parts, *before)


def prep_kernel(count, place, raw_t, bias, rate, seg_row, seg_col, *refs):
    quarters, (bc_t, c_seg, tail_t, run, run_t, step_t) = refs[:count], refs[-6:]
    heads, num_tok = raw_t.shape
    share = quarters[0].shape[0]
    dim = bc_t.shape[0] // 2
    for k, quarter in enumerate(quarters):
        at = lax.rem(place[4] - k + count, count) * share
        bc_t[pl.ds(pl.multiple_of(at, share), share), :] = quarter[...]
    z = raw_t[...] + bias[...]
    step = jnp.maximum(z, 0.0) + jnp.log1p(jnp.exp(-jnp.abs(z)))
    log_decay = -step * rate[...]
    down = lax.broadcasted_iota(jnp.int32, (num_tok, num_tok), 0)
    along = lax.broadcasted_iota(jnp.int32, (num_tok, num_tok), 1)
    same = seg_row[...] == seg_col[...]
    causal = (same & (down >= along)).astype(F32)
    run[...] = dot32(causal, log_decay, NT)
    running = dot32(log_decay, causal, NT)
    totals = dot32(log_decay, same.astype(F32), NT)
    run_t[...] = running
    step_t[...] = step
    grown = jnp.exp(totals)
    high = grown.astype(BF)
    tail_t[...] = jnp.zeros_like(tail_t)
    tail_t[:heads, :] = (jnp.exp(jnp.minimum(totals - running, 0.0)) * step).astype(BF)
    tail_t[16 : 16 + heads, :] = high
    tail_t[32 : 32 + heads, :] = (grown - high.astype(F32)).astype(BF)
    seg_rows = jnp.broadcast_to(seg_col[...].astype(F32), (16, num_tok)).astype(BF)
    tail_t[48:64, :] = seg_rows
    c_seg[:dim, :] = bc_t[dim:, :]
    c_seg[dim:, :] = seg_rows


def prep(place, raw_t, bias, rate, seg, quarters, before):
    heads, num_tok = raw_t.shape
    rows = quarters[0].shape[0] * len(quarters)
    vmem = pl.BlockSpec(memory_space=pltpu.VMEM)
    return pl.pallas_call(
        functools.partial(prep_kernel, len(quarters)),
        out_shape=[
            jax.ShapeDtypeStruct((rows, num_tok), BF),
            jax.ShapeDtypeStruct((rows // 2 + 16, num_tok), BF),
            jax.ShapeDtypeStruct((64, num_tok), BF),
            jax.ShapeDtypeStruct((num_tok, heads), F32),
            jax.ShapeDtypeStruct((heads, num_tok), F32),
            jax.ShapeDtypeStruct((heads, num_tok), F32),
        ],
        in_specs=[pl.BlockSpec(memory_space=pltpu.SMEM)]
        + [vmem] * (5 + len(quarters))
        + [pl.BlockSpec(memory_space=pl.ANY)] * len(before),
        compiler_params=PARAMS,
        cost_estimate=COST,
    )(place, raw_t, bias[:, None], rate[:, None], seg[:, None], seg[None, :], *quarters, *before)


def carried_kernel(owners, ranks, slot, member, *refs):
    c_segs, outs = refs[:owners], refs[-owners:]
    states = refs[owners : owners + ranks]
    heads, width, dim = states[0].shape[1:]
    at = pl.program_id(0)
    flat = [state[0].reshape(heads * width, dim).astype(BF) for state in states]

    def fill(c_seg, out):
        c_rows = c_seg[:dim, :].astype(F32)
        seg = c_seg[dim : dim + 1, :].astype(F32)
        total = jnp.zeros(out.shape, F32)
        for rank in range(ranks):
            inside = seg == member[at * ranks + rank].astype(F32)
            mine = jnp.where(inside, c_rows, 0.0).T.astype(BF)
            total += dot16(mine, flat[rank], NT)
        out[...] = total.astype(BF)

    for i in range(owners):
        pl.when(at == i)(functools.partial(fill, c_segs[i], outs[i]))


def carried_part(slot, member, c_segs, cache, before):
    num_tok = c_segs[0].shape[1]
    _, heads, width, dim = cache.shape
    owners = len(c_segs)
    ranks = slot.shape[0] // owners

    def state_map(rank, i, slot, member):
        return (slot[i * ranks + rank], 0, 0, 0)

    return pl.pallas_call(
        functools.partial(carried_kernel, owners, ranks),
        out_shape=[jax.ShapeDtypeStruct((num_tok, heads * width), BF)] * owners,
        grid_spec=pltpu.PrefetchScalarGridSpec(
            num_scalar_prefetch=2,
            grid=(owners,),
            in_specs=[pl.BlockSpec(c_seg.shape, lambda i, *_: (0, 0)) for c_seg in c_segs]
            + [
                pl.BlockSpec((1, heads, width, dim), functools.partial(state_map, rank))
                for rank in range(ranks)
            ]
            + [pl.BlockSpec(memory_space=pl.ANY)] * len(before),
            out_specs=[pl.BlockSpec((num_tok, heads * width), lambda i, *_: (0, 0))] * owners,
        ),
        compiler_params=PARAMS,
        cost_estimate=COST,
    )(slot, member, *c_segs, *([cache] * ranks), *before)


def gather_kernel(count, *refs):
    parts = refs[:count]
    bc_t, tail_t = refs[count : count + 2]
    x, bundle = refs[-2:]
    columns = x.shape[1]
    dim = bc_t.shape[0] // 2
    for first in range(0, columns, LANES):
        at = slice(first, first + LANES)
        total = parts[0][:, at].astype(F32)
        for part in parts[1:]:
            total += part[:, at].astype(F32)
        x[:, at] = total.astype(BF)
        bundle[at, :] = total.T.astype(BF)
    bundle[columns : columns + dim, :] = bc_t[:dim, :]
    bundle[columns + dim :, :] = tail_t[...]


def gather_part(parts, bc_t, tail_t, before):
    num_tok, columns = parts[0].shape
    rows = columns + bc_t.shape[0] // 2 + tail_t.shape[0]
    vmem = pl.BlockSpec(memory_space=pltpu.VMEM)
    return pl.pallas_call(
        functools.partial(gather_kernel, len(parts)),
        out_shape=[
            jax.ShapeDtypeStruct((num_tok, columns), BF),
            jax.ShapeDtypeStruct((rows, num_tok), BF),
        ],
        in_specs=[vmem] * (len(parts) + 2) + [pl.BlockSpec(memory_space=pl.ANY)] * len(before),
        compiler_params=PARAMS,
        cost_estimate=COST,
    )(*parts, bc_t, tail_t, *before)


def within_kernel(x, bc_t, seg_row, seg_col, run, run_t, step_t, gain, base, grown):
    num_tok, columns = base.shape
    heads = run.shape[1]
    width = columns // heads
    down = lax.broadcasted_iota(jnp.int32, (num_tok, num_tok), 0)
    along = lax.broadcasted_iota(jnp.int32, (num_tok, num_tok), 1)
    keep = (seg_row[...] == seg_col[...]) & (down >= along)
    dim = bc_t.shape[0] // 2
    raw = dot16(bc_t[dim:, :], bc_t[:dim, :], TN)
    scores = jnp.where(keep, raw, 0.0)
    pair = LANES // width
    lane = lax.broadcasted_iota(jnp.int32, (num_tok, LANES), 1) // width
    for first in range(0, heads, pair):
        at = slice(first * width, (first + pair) * width)
        values = x[:, at]
        exact = values.astype(F32)
        total = jnp.zeros((num_tok, LANES), F32)
        rise = jnp.zeros((num_tok, LANES), F32)
        for i in range(pair):
            h = first + i
            run_col = run[:, h : h + 1]
            decay = jnp.exp(jnp.minimum(run_col - run_t[h : h + 1, :], 0.0))
            mixing = (decay * scores * step_t[h : h + 1, :]).astype(BF)
            inner = dot16(mixing, values, NN) + gain[:, h : h + 1] * exact
            total = jnp.where(lane == i, inner, total)
            rise = jnp.where(lane == i, jnp.exp(run_col), rise)
        base[:, at] = total
        grown[:, at] = rise


def within_part(x, bc_t, seg, run, run_t, step_t, gain):
    num_tok, columns = x.shape
    heads = run.shape[1]
    return pl.pallas_call(
        within_kernel,
        out_shape=[jax.ShapeDtypeStruct((num_tok, columns), F32)] * 2,
        compiler_params=PARAMS,
        cost_estimate=COST,
    )(x, bc_t, seg[:, None], seg[None, :], run, run_t, step_t, gain[None])


def outputs_kernel(count, base, grown, *refs):
    held = refs[0][...].astype(F32)
    for block in refs[1:count]:
        held += block[...].astype(F32)
    refs[-1][...] = (base[...] + grown[...] * held).astype(BF)


def outputs_part(base, grown, carried, before):
    vmem = pl.BlockSpec(memory_space=pltpu.VMEM)
    rest = pl.BlockSpec(memory_space=pl.ANY)
    return pl.pallas_call(
        functools.partial(outputs_kernel, len(carried)),
        out_shape=jax.ShapeDtypeStruct(base.shape, BF),
        in_specs=[vmem] * (2 + len(carried)) + [rest] * len(before),
        compiler_params=PARAMS,
        cost_estimate=COST,
    )(base, grown, *carried, *before)


def states_kernel(sources, which, member, state, *refs):
    bundles, (out, done) = refs[:sources], refs[-2:]
    heads, width, dim = state.shape[1:]
    columns = heads * width
    at = pl.program_id(0)
    done[...] = jnp.zeros_like(done)

    def update(bundle):
        b_rows = bundle[columns : columns + dim, :]
        tail = bundle[columns + dim :, :].astype(F32)
        inside = tail[48:49] == member[at].astype(F32)
        weights = jnp.where(inside, tail[:heads], 0.0)
        rise = tail[16 : 16 + heads] + tail[32 : 32 + heads]
        rise = jnp.max(jnp.where(inside, rise, 0.0), axis=1, keepdims=True)
        for h in range(heads):
            rows = slice(h * width, (h + 1) * width)
            scaled = (bundle[rows, :].astype(F32) * weights[h : h + 1]).astype(BF)
            out[0, h] = state[0, h] * rise[h : h + 1] + dot16(scaled, b_rows, NT)

    for i in range(sources):
        pl.when(which[at] == i)(functools.partial(update, bundles[i]))

    @pl.when(which[at] < 0)
    def _():
        out[...] = state[...]


def states_part(which, member, cache, bundles, before):
    slots, heads, width, dim = cache.shape
    rows, num_tok = bundles[0].shape
    slab = pl.BlockSpec((1, heads, width, dim), lambda s, *_: (s, 0, 0, 0))
    fixed = pl.BlockSpec((rows, num_tok), lambda s, *_: (0, 0))
    return pl.pallas_call(
        functools.partial(states_kernel, len(bundles)),
        out_shape=[
            jax.ShapeDtypeStruct(cache.shape, cache.dtype),
            jax.ShapeDtypeStruct((8, LANES), jnp.int32),
        ],
        grid_spec=pltpu.PrefetchScalarGridSpec(
            num_scalar_prefetch=2,
            grid=(slots,),
            in_specs=[slab]
            + [fixed] * len(bundles)
            + [pl.BlockSpec(memory_space=pl.ANY)] * len(before),
            out_specs=[slab, pl.BlockSpec((8, LANES), lambda s, *_: (0, 0))],
        ),
        compiler_params=PARAMS,
        cost_estimate=COST,
    )(which, member, cache, *bundles, *before)


def output_kernel(count, place, w_out, *refs):
    blocks, (kept, given, product) = refs[:count], refs[-3:]
    half = product.shape[0] // 2
    for i, block in enumerate(blocks):
        product[...] = dot16(block[...], w_out[...], NN).astype(BF)
        rows = slice(i * half, (i + 1) * half)
        kept[rows, :] = product[pl.ds(pl.multiple_of(place[1] * half, half), half), :]
        given[rows, :] = product[pl.ds(pl.multiple_of((1 - place[1]) * half, half), half), :]


def output_part(place, w_out, blocks, before):
    vmem = pl.BlockSpec(memory_space=pltpu.VMEM)
    num_tok, columns = blocks[0].shape[0], w_out.shape[1]
    half = jax.ShapeDtypeStruct((len(blocks) * num_tok // 2, columns), BF)
    return pl.pallas_call(
        functools.partial(output_kernel, len(blocks)),
        out_shape=[half, half],
        in_specs=[pl.BlockSpec(memory_space=pltpu.SMEM)]
        + [vmem] * (1 + len(blocks))
        + [pl.BlockSpec(memory_space=pl.ANY)] * len(before),
        scratch_shapes=[pltpu.VMEM((num_tok, columns), BF)],
        compiler_params=PARAMS,
        cost_estimate=COST,
    )(place, w_out, *blocks, *before)


def core_kernel(count, half, place, kept, got, *refs):
    mine, *theirs, total = refs
    chips = 1 + len(theirs)
    share = half // chips
    total[...] = (kept[...].astype(F32) + got[...].astype(F32)).astype(BF)
    for turn, out in enumerate((mine, *theirs)):
        at = lax.rem(place[0] + turn, chips) * share
        for i in range(count):
            rows = pl.ds(pl.multiple_of(i * half + at, share), share)
            out[i * share : (i + 1) * share, :] = total[rows, :]


def core_part(place, kept, got, chips, half):
    vmem = pl.BlockSpec(memory_space=pltpu.VMEM)
    rows, columns = kept.shape
    share = jax.ShapeDtypeStruct((rows // chips, columns), BF)
    mine, *theirs = pl.pallas_call(
        functools.partial(core_kernel, rows // half, half),
        out_shape=[share] * chips,
        in_specs=[pl.BlockSpec(memory_space=pltpu.SMEM), vmem, vmem],
        scratch_shapes=[pltpu.VMEM((rows, columns), BF)],
        compiler_params=PARAMS,
        cost_estimate=COST,
    )(place, kept, got)
    return mine, theirs


def chip_kernel(count, others, mine, *refs):
    theirs, outs = refs[:others], refs[-count:]
    share = mine.shape[0] // count
    for i, out in enumerate(outs):
        rows = slice(i * share, (i + 1) * share)
        total = mine[rows, :].astype(F32)
        for block in theirs:
            total += block[rows, :].astype(F32)
        out[...] = total.astype(BF)


def chip_part(mine, theirs, count, before):
    rows, columns = mine.shape
    vmem = pl.BlockSpec(memory_space=pltpu.VMEM)
    return pl.pallas_call(
        functools.partial(chip_kernel, count, len(theirs)),
        out_shape=[jax.ShapeDtypeStruct((rows // count, columns), BF)] * count,
        in_specs=[vmem] * (1 + len(theirs)) + [pl.BlockSpec(memory_space=pl.ANY)] * len(before),
        compiler_params=PARAMS,
        cost_estimate=COST,
    )(mine, *theirs, *before)


def order_kernel(count, place, *refs):
    out = refs[-1]
    rows = refs[0].shape[0]
    for k in range(count):
        source = lax.rem(place[4] - k + count, count)
        at = (lax.rem(source, 2) * (count // 2) + lax.div(source, 2)) * rows
        out[pl.ds(pl.multiple_of(at, rows), rows), :] = refs[k][...]


def order_part(place, shares):
    vmem = pl.BlockSpec(memory_space=pltpu.VMEM)
    rows, columns = shares[0].shape
    return pl.pallas_call(
        functools.partial(order_kernel, len(shares)),
        out_shape=jax.ShapeDtypeStruct((rows * len(shares), columns), BF),
        in_specs=[pl.BlockSpec(memory_space=pltpu.SMEM)] + [vmem] * len(shares),
        compiler_params=PARAMS,
        cost_estimate=COST,
    )(place, *shares)


def body(
    tokens,
    w_x,
    w_bc,
    w_dt,
    dt_bias,
    decay_rate,
    skip_gain,
    w_out,
    suffix_lengths,
    checkpoint_slot,
    cache,
):
    reqs = lax.axis_size("req")
    tensors = lax.axis_size("tensor")
    chips = tensors // 2
    own_req = lax.axis_index("req")
    own_tensor = lax.axis_index("tensor")
    own_chip = own_tensor // 2
    core = own_tensor % 2
    num_tok = tokens.shape[0]
    depth = w_x.shape[0]
    slots_dev, heads, width, state_dim = cache.shape
    columns = heads * width
    half = depth // 2
    piece = num_tok // chips
    piece = num_tok // chips

    places = jnp.arange(num_tok, dtype=jnp.int32)
    ends = jnp.cumsum(suffix_lengths[0])
    seg = jnp.sum((places[:, None] >= ends[None, :]).astype(jnp.int32), axis=1)

    share = w_bc.shape[1] // tensors
    bc_share = lax.dynamic_slice_in_dim(w_bc, own_tensor * share, share, axis=1)
    w_small = jnp.concatenate(
        [bc_share, w_dt, w_dt, jnp.zeros((depth, LANES - share - 2 * heads), BF)], axis=1
    )
    place = jnp.stack(
        [own_chip, core, 0 * core + share + heads, 0 * core + share + 2 * heads, own_tensor]
    ).astype(jnp.int32)
    own_block = lax.dynamic_slice(tokens, (0, own_req * depth), (num_tok, depth))
    parts = [jnp.dot(own_block, w_x, preferred_element_type=F32).astype(BF)]
    smalls = [jnp.dot(own_block, w_small, preferred_element_type=F32)]
    order = sorted(range(1, reqs), key=lambda k: min(k, reqs - k))
    blocks, own_smalls = [], []
    for k in order:
        start = ((own_req + k) % reqs) * depth + core * half
        block = lax.dynamic_slice(tokens, (own_chip * piece, start), (piece, half))
        block = turn_req(block, k)
        near = [block] + [turn_chip(block, turn) for turn in range(1, chips)]
        block, small = block_part(place, w_small, near, [swap_core(b) for b in near])
        blocks.append(block)
        own_smalls.append(small)
        smalls.append(turn_req(small, -k))
    products = [product_part(blocks[0], w_x, [])]
    for i, block in enumerate(blocks[1:], 1):
        before = [smalls[1], own_smalls[-1]] if i < len(blocks) - 1 else smalls[2:]
        products.append(product_part(block, w_x, before))
    parts += [turn_req(product, -k) for k, product in zip(order, products)]

    bc_share, raw_t = fold_part(smalls[0], smalls[1:], share, heads, [])
    quarters = [bc_share] + [turn_tensor(bc_share, k) for k in range(1, tensors)]
    bc_t, c_seg, tail_t, run, run_t, step_t = prep(
        place, raw_t, dt_bias, decay_rate, seg, quarters, [parts[1], *products[1:]]
    )
    c_segs = [c_seg] + [turn_req(c_seg, k) for k in range(1, reqs)]
    x, bundle = gather_part(parts, bc_t, tail_t, [])
    below, above = line_gather(bundle)

    per_pair = (slots_dev + reqs - 1) // reqs
    total_reqs = checkpoint_slot.shape[0]
    req_dev = total_reqs // reqs
    holder = checkpoint_slot // slots_dev
    index = jnp.arange(total_reqs, dtype=jnp.int32)
    owner = index // req_dev
    pair_key = holder * reqs + owner
    rank_in_pair = jnp.sum(
        (pair_key[:, None] == pair_key[None, :])
        & (checkpoint_slot[None, :] < checkpoint_slot[:, None]),
        axis=1,
    )
    away = (own_req - owner) % reqs
    pairs = jnp.arange(reqs * per_pair, dtype=jnp.int32)
    match = (holder == own_req)[None, :] & (
        (away * per_pair + rank_in_pair)[None, :] == pairs[:, None]
    )

    def pick(match, values, missing):
        found = jnp.sum(jnp.where(match, values[None, :], 0), axis=1)
        return jnp.where(jnp.any(match, axis=1), found, missing).astype(jnp.int32)

    pair_slot = pick(match, checkpoint_slot % slots_dev, 0)
    pair_member = pick(match, index % req_dev, -1)

    carried = carried_part(pair_slot, pair_member, c_segs, cache, [])

    base, grown = within_part(x, bc_t, seg, run, run_t, step_t, skip_gain)
    outputs = outputs_part(base, grown, line_sum(carried), [below[-1], above[-1]])

    slot_ids = own_req * slots_dev + jnp.arange(slots_dev, dtype=jnp.int32)
    match_slot = checkpoint_slot[None, :] == slot_ids[:, None]
    which = jnp.where(owner <= own_req, own_req - owner, reqs - 1 + owner - own_req)

    def sum_cores(kept, given):
        mine, theirs = core_part(place, kept, swap_core(given), chips, num_tok // 2)
        return mine, [turn_chip(block, turn + 1) for turn, block in enumerate(theirs)]

    far = order[-1]
    came = {k: turn_req(outputs, k) for k in order}
    kept, given = output_part(place, w_out, [outputs, came[far]], [])
    new_cache, zero = states_part(
        pick(match_slot, which, -1),
        pick(match_slot, index % req_dev, -1),
        cache,
        [bundle, *below, *above],
        [kept],
    )
    arrived = {}
    arrived[0], block = chip_part(*sum_cores(kept, given), 2, [])
    arrived[far] = turn_req(block, -far)
    kept, given = output_part(place, w_out, [came[k] for k in order[:-1]], [zero, block])
    blocks = chip_part(*sum_cores(kept, given), reqs - 2, [arrived[far]])
    for k, block in zip(order, blocks):
        arrived[k] = turn_req(block, -k)

    def column_block(req):
        chosen = arrived[0]
        for k in range(1, reqs):
            chosen = jnp.where((req - own_req) % reqs == k, arrived[k], chosen)
        return chosen

    shares = [column_block(own_tensor)]
    for k in range(1, tensors):
        block = column_block((own_tensor + k) % tensors)
        shares.append(
            lax.ppermute(block, "tensor", [(i, (i + k) % tensors) for i in range(tensors)])
        )
    layer_out = order_part(place, shares)
    return (layer_out, new_cache)


def solution(mesh):
    placed = (
        P(("groups", "req"), None),
        P("req", "tensor"),
        P("req", None),
        P("req", "tensor"),
        P("tensor"),
        P("tensor"),
        P("tensor"),
        P("tensor", "req"),
        P(("groups", "req"), None),
        P("groups"),
        P(("groups", "req"), "tensor", None, None),
    )
    return jax.shard_map(
        body,
        mesh=mesh,
        in_specs=placed,
        out_specs=(P(("groups", "req"), "tensor"), P(("groups", "req"), "tensor", None, None)),
        check_vma=False,
    )
```

```python
import functools

import jax
import jax.numpy as jnp
from jax import lax
from jax.experimental import pallas as pl
from jax.experimental.pallas import tpu as pltpu
from jax.sharding import PartitionSpec as P

HIGH = lax.Precision.HIGHEST
BF = jnp.bfloat16
F32 = jnp.float32
NN = (((1,), (0,)), ((), ()))
NT = (((1,), (1,)), ((), ()))
TN = (((0,), (0,)), ((), ()))
TT = (((0,), (1,)), ((), ()))
LANES = 128
PARAMS = pltpu.CompilerParams(vmem_limit_bytes=24 * 1024 * 1024)
COST = pl.CostEstimate(flops=1, bytes_accessed=1, transcendentals=0)


def turn_req(x, turn):
    count = lax.axis_size("req")
    return lax.ppermute(x, "req", [(i, (i + turn) % count) for i in range(count)])


def step_up(x, first, last):
    return lax.ppermute(x, "req", [(i, i + 1) for i in range(first, last)])


def step_down(x, first, last):
    top = lax.axis_size("req") - 1
    return lax.ppermute(x, "req", [(top - i, top - i - 1) for i in range(first, last)])


def line_gather(x):
    count = lax.axis_size("req")
    below, above = [], []
    low = high = x
    for hop in range(count - 1):
        low, high = step_up(low, hop, count - 1), step_down(high, hop, count - 1)
        below.append(low)
        above.append(high)
    return below, above


def line_sum(blocks):
    count = lax.axis_size("req")
    low, high = blocks[1], blocks[count - 1]
    for hop in range(1, count):
        if hop > 1:
            low, high = low + blocks[hop], high + blocks[count - hop]
        low, high = step_up(low, 0, hop), step_down(high, 0, hop)
    return blocks[0], low, high


def swap_core(x):
    count = lax.axis_size("tensor")
    return lax.ppermute(x, "tensor", [(i, i ^ 1) for i in range(count)])


def turn_chip(x, turn):
    count = lax.axis_size("tensor")
    return lax.ppermute(x, "tensor", [(i, (i + 2 * turn) % count) for i in range(count)])


def turn_tensor(x, turn):
    count = lax.axis_size("tensor")
    return lax.ppermute(x, "tensor", [(i, (i + turn) % count) for i in range(count)])


def dot32(a, b, dims):
    return lax.dot_general(a, b, dims, precision=HIGH, preferred_element_type=F32)


def dot16(a, b, dims):
    return lax.dot_general(a, b, dims, preferred_element_type=F32)


def block_kernel(chips, place, w_small, *refs):
    near, far, (block, small) = refs[:chips], refs[chips : 2 * chips], refs[-2:]
    piece, half = near[0].shape

    def fill(core):
        own, other = slice(core * half, (core + 1) * half), slice((1 - core) * half, (2 - core) * half)
        for i in range(chips):
            at = lax.rem(place[0] - i + chips, chips) * piece
            rows = pl.ds(pl.multiple_of(at, piece), piece)
            block[rows, own] = near[i][...]
            block[rows, other] = far[i][...]

    for core in range(2):
        pl.when(place[1] == core)(functools.partial(fill, core))
    sums = dot16(block[...], w_small[...], NN)
    lane = lax.broadcasted_iota(jnp.int32, sums.shape, 1)
    low = (lane >= place[2]) & (lane < place[3])
    high = sums.astype(BF)
    small[...] = jnp.where(low, sums - high.astype(F32), sums).astype(BF)


def block_part(place, w_small, near, far, before):
    chips = len(near)
    num_tok = near[0].shape[0] * chips
    vmem = pl.BlockSpec(memory_space=pltpu.VMEM)
    return pl.pallas_call(
        functools.partial(block_kernel, chips),
        out_shape=[
            jax.ShapeDtypeStruct((num_tok, w_small.shape[0]), BF),
            jax.ShapeDtypeStruct((num_tok, LANES), BF),
        ],
        in_specs=[pl.BlockSpec(memory_space=pltpu.SMEM)]
        + [vmem] * (1 + 2 * chips)
        + [pl.BlockSpec(memory_space=pl.ANY)] * len(before),
        compiler_params=PARAMS,
        cost_estimate=COST,
    )(place, w_small, *near, *far, *before)


def product_kernel(block, weights, *refs):
    refs[-1][...] = dot16(block[...], weights[...], NN).astype(BF)


def product_part(block, weights, before):
    vmem = pl.BlockSpec(memory_space=pltpu.VMEM)
    return pl.pallas_call(
        product_kernel,
        out_shape=jax.ShapeDtypeStruct((block.shape[0], weights.shape[1]), BF),
        in_specs=[vmem, vmem] + [pl.BlockSpec(memory_space=pl.ANY)] * len(before),
        compiler_params=PARAMS,
        cost_estimate=COST,
    )(block, weights, *before)


def fold_kernel(share, heads, count, own, *refs):
    parts, (bc_t, raw_t) = refs[:count], refs[-2:]
    lane = lax.broadcasted_iota(jnp.int32, own.shape, 1)
    total = jnp.where(lane < share + heads, own[...], 0.0)
    for part in parts:
        total += part[...].astype(F32)
    total = total.T
    bc_t[...] = total[:share].astype(BF)
    raw_t[...] = total[share : share + heads] + total[share + heads : share + 2 * heads]


def fold_part(own, parts, share, heads, before):
    num_tok = own.shape[0]
    vmem = pl.BlockSpec(memory_space=pltpu.VMEM)
    rest = pl.BlockSpec(memory_space=pl.ANY)
    return pl.pallas_call(
        functools.partial(fold_kernel, share, heads, len(parts)),
        out_shape=[
            jax.ShapeDtypeStruct((share, num_tok), BF),
            jax.ShapeDtypeStruct((heads, num_tok), F32),
        ],
        in_specs=[vmem] * (1 + len(parts)) + [rest] * len(before),
        compiler_params=PARAMS,
        cost_estimate=COST,
    )(own, *parts, *before)


def prep_kernel(count, place, raw_t, bias, rate, seg_row, seg_col, *refs):
    quarters, (bc_t, c_seg, tail_t, run, run_t, step_t) = refs[:count], refs[-6:]
    heads, num_tok = raw_t.shape
    share = quarters[0].shape[0]
    dim = bc_t.shape[0] // 2
    for k, quarter in enumerate(quarters):
        at = lax.rem(place[4] - k + count, count) * share
        bc_t[pl.ds(pl.multiple_of(at, share), share), :] = quarter[...]
    z = raw_t[...] + bias[...]
    step = jnp.maximum(z, 0.0) + jnp.log1p(jnp.exp(-jnp.abs(z)))
    log_decay = -step * rate[...]
    down = lax.broadcasted_iota(jnp.int32, (num_tok, num_tok), 0)
    along = lax.broadcasted_iota(jnp.int32, (num_tok, num_tok), 1)
    same = seg_row[...] == seg_col[...]
    causal = (same & (down >= along)).astype(F32)
    run[...] = dot32(causal, log_decay, NT)
    running = dot32(log_decay, causal, NT)
    totals = dot32(log_decay, same.astype(F32), NT)
    run_t[...] = running
    step_t[...] = step
    grown = jnp.exp(totals)
    high = grown.astype(BF)
    tail_t[...] = jnp.zeros_like(tail_t)
    tail_t[:heads, :] = (jnp.exp(jnp.minimum(totals - running, 0.0)) * step).astype(BF)
    tail_t[16 : 16 + heads, :] = high
    tail_t[32 : 32 + heads, :] = (grown - high.astype(F32)).astype(BF)
    seg_rows = jnp.broadcast_to(seg_col[...].astype(F32), (16, num_tok)).astype(BF)
    tail_t[48:64, :] = seg_rows
    c_seg[:dim, :] = bc_t[dim:, :]
    c_seg[dim:, :] = seg_rows


def prep(place, raw_t, bias, rate, seg, quarters, before):
    heads, num_tok = raw_t.shape
    rows = quarters[0].shape[0] * len(quarters)
    vmem = pl.BlockSpec(memory_space=pltpu.VMEM)
    return pl.pallas_call(
        functools.partial(prep_kernel, len(quarters)),
        out_shape=[
            jax.ShapeDtypeStruct((rows, num_tok), BF),
            jax.ShapeDtypeStruct((rows // 2 + 16, num_tok), BF),
            jax.ShapeDtypeStruct((64, num_tok), BF),
            jax.ShapeDtypeStruct((num_tok, heads), F32),
            jax.ShapeDtypeStruct((heads, num_tok), F32),
            jax.ShapeDtypeStruct((heads, num_tok), F32),
        ],
        in_specs=[pl.BlockSpec(memory_space=pltpu.SMEM)]
        + [vmem] * (5 + len(quarters))
        + [pl.BlockSpec(memory_space=pl.ANY)] * len(before),
        compiler_params=PARAMS,
        cost_estimate=COST,
    )(place, raw_t, bias[:, None], rate[:, None], seg[:, None], seg[None, :], *quarters, *before)


def carried_kernel(owners, ranks, slot, member, *refs):
    c_segs, outs = refs[:owners], refs[-owners:]
    states = refs[owners : owners + ranks]
    heads, width, dim = states[0].shape[1:]
    at = pl.program_id(0)
    flat = [state[0].reshape(heads * width, dim).astype(BF) for state in states]

    def fill(c_seg, out):
        c_rows = c_seg[:dim, :].astype(F32)
        seg = c_seg[dim : dim + 1, :].astype(F32)
        total = jnp.zeros(out.shape, F32)
        for rank in range(ranks):
            inside = seg == member[at * ranks + rank].astype(F32)
            mine = jnp.where(inside, c_rows, 0.0).T.astype(BF)
            total += dot16(mine, flat[rank], NT)
        out[...] = total.astype(BF)

    for i in range(owners):
        pl.when(at == i)(functools.partial(fill, c_segs[i], outs[i]))


def carried_part(slot, member, c_segs, cache, before):
    num_tok = c_segs[0].shape[1]
    _, heads, width, dim = cache.shape
    owners = len(c_segs)
    ranks = slot.shape[0] // owners

    def state_map(rank, i, slot, member):
        return (slot[i * ranks + rank], 0, 0, 0)

    return pl.pallas_call(
        functools.partial(carried_kernel, owners, ranks),
        out_shape=[jax.ShapeDtypeStruct((num_tok, heads * width), BF)] * owners,
        grid_spec=pltpu.PrefetchScalarGridSpec(
            num_scalar_prefetch=2,
            grid=(owners,),
            in_specs=[pl.BlockSpec(c_seg.shape, lambda i, *_: (0, 0)) for c_seg in c_segs]
            + [
                pl.BlockSpec((1, heads, width, dim), functools.partial(state_map, rank))
                for rank in range(ranks)
            ]
            + [pl.BlockSpec(memory_space=pl.ANY)] * len(before),
            out_specs=[pl.BlockSpec((num_tok, heads * width), lambda i, *_: (0, 0))] * owners,
        ),
        compiler_params=PARAMS,
        cost_estimate=COST,
    )(slot, member, *c_segs, *([cache] * ranks), *before)


def gather_kernel(count, *refs):
    parts = refs[:count]
    bc_t, tail_t = refs[count : count + 2]
    x, bundle = refs[-2:]
    columns = x.shape[1]
    dim = bc_t.shape[0] // 2
    for first in range(0, columns, LANES):
        at = slice(first, first + LANES)
        total = parts[0][:, at].astype(F32)
        for part in parts[1:]:
            total += part[:, at].astype(F32)
        x[:, at] = total.astype(BF)
        bundle[at, :] = total.T.astype(BF)
    bundle[columns : columns + dim, :] = bc_t[:dim, :]
    bundle[columns + dim :, :] = tail_t[...]


def gather_part(parts, bc_t, tail_t, before):
    num_tok, columns = parts[0].shape
    rows = columns + bc_t.shape[0] // 2 + tail_t.shape[0]
    vmem = pl.BlockSpec(memory_space=pltpu.VMEM)
    return pl.pallas_call(
        functools.partial(gather_kernel, len(parts)),
        out_shape=[
            jax.ShapeDtypeStruct((num_tok, columns), BF),
            jax.ShapeDtypeStruct((rows, num_tok), BF),
        ],
        in_specs=[vmem] * (len(parts) + 2) + [pl.BlockSpec(memory_space=pl.ANY)] * len(before),
        compiler_params=PARAMS,
        cost_estimate=COST,
    )(*parts, bc_t, tail_t, *before)


def within_kernel(x, bc_t, seg_row, seg_col, run, run_t, step_t, gain, base, grown):
    num_tok, columns = base.shape
    heads = run.shape[1]
    width = columns // heads
    down = lax.broadcasted_iota(jnp.int32, (num_tok, num_tok), 0)
    along = lax.broadcasted_iota(jnp.int32, (num_tok, num_tok), 1)
    keep = (seg_row[...] == seg_col[...]) & (down >= along)
    dim = bc_t.shape[0] // 2
    raw = dot16(bc_t[dim:, :], bc_t[:dim, :], TN)
    scores = jnp.where(keep, raw, 0.0)
    pair = LANES // width
    lane = lax.broadcasted_iota(jnp.int32, (num_tok, LANES), 1) // width
    for first in range(0, heads, pair):
        at = slice(first * width, (first + pair) * width)
        values = x[:, at]
        exact = values.astype(F32)
        total = jnp.zeros((num_tok, LANES), F32)
        rise = jnp.zeros((num_tok, LANES), F32)
        for i in range(pair):
            h = first + i
            run_col = run[:, h : h + 1]
            decay = jnp.exp(jnp.minimum(run_col - run_t[h : h + 1, :], 0.0))
            mixing = (decay * scores * step_t[h : h + 1, :]).astype(BF)
            inner = dot16(mixing, values, NN) + gain[:, h : h + 1] * exact
            total = jnp.where(lane == i, inner, total)
            rise = jnp.where(lane == i, jnp.exp(run_col), rise)
        base[:, at] = total
        grown[:, at] = rise


def within_part(x, bc_t, seg, run, run_t, step_t, gain):
    num_tok, columns = x.shape
    heads = run.shape[1]
    return pl.pallas_call(
        within_kernel,
        out_shape=[jax.ShapeDtypeStruct((num_tok, columns), F32)] * 2,
        compiler_params=PARAMS,
        cost_estimate=COST,
    )(x, bc_t, seg[:, None], seg[None, :], run, run_t, step_t, gain[None])


def outputs_kernel(count, base, grown, *refs):
    held = refs[0][...].astype(F32)
    for block in refs[1:count]:
        held += block[...].astype(F32)
    refs[-1][...] = (base[...] + grown[...] * held).astype(BF)


def outputs_part(base, grown, carried, before):
    vmem = pl.BlockSpec(memory_space=pltpu.VMEM)
    rest = pl.BlockSpec(memory_space=pl.ANY)
    return pl.pallas_call(
        functools.partial(outputs_kernel, len(carried)),
        out_shape=jax.ShapeDtypeStruct(base.shape, BF),
        in_specs=[vmem] * (2 + len(carried)) + [rest] * len(before),
        compiler_params=PARAMS,
        cost_estimate=COST,
    )(base, grown, *carried, *before)


def states_kernel(sources, which, member, state, *refs):
    bundles, (out, done) = refs[:sources], refs[-2:]
    heads, width, dim = state.shape[1:]
    columns = heads * width
    at = pl.program_id(0)
    done[...] = jnp.zeros_like(done)

    def update(bundle):
        b_rows = bundle[columns : columns + dim, :]
        tail = bundle[columns + dim :, :].astype(F32)
        inside = tail[48:49] == member[at].astype(F32)
        weights = jnp.where(inside, tail[:heads], 0.0)
        rise = tail[16 : 16 + heads] + tail[32 : 32 + heads]
        rise = jnp.max(jnp.where(inside, rise, 0.0), axis=1, keepdims=True)
        for h in range(heads):
            rows = slice(h * width, (h + 1) * width)
            scaled = (bundle[rows, :].astype(F32) * weights[h : h + 1]).astype(BF)
            out[0, h] = state[0, h] * rise[h : h + 1] + dot16(scaled, b_rows, NT)

    for i in range(sources):
        pl.when(which[at] == i)(functools.partial(update, bundles[i]))

    @pl.when(which[at] < 0)
    def _():
        out[...] = state[...]


def states_part(which, member, cache, bundles, before):
    slots, heads, width, dim = cache.shape
    rows, num_tok = bundles[0].shape
    slab = pl.BlockSpec((1, heads, width, dim), lambda s, *_: (s, 0, 0, 0))
    fixed = pl.BlockSpec((rows, num_tok), lambda s, *_: (0, 0))
    return pl.pallas_call(
        functools.partial(states_kernel, len(bundles)),
        out_shape=[
            jax.ShapeDtypeStruct(cache.shape, cache.dtype),
            jax.ShapeDtypeStruct((8, LANES), jnp.int32),
        ],
        grid_spec=pltpu.PrefetchScalarGridSpec(
            num_scalar_prefetch=2,
            grid=(slots,),
            in_specs=[slab]
            + [fixed] * len(bundles)
            + [pl.BlockSpec(memory_space=pl.ANY)] * len(before),
            out_specs=[slab, pl.BlockSpec((8, LANES), lambda s, *_: (0, 0))],
        ),
        compiler_params=PARAMS,
        cost_estimate=COST,
    )(which, member, cache, *bundles, *before)


def output_kernel(count, place, w_out, *refs):
    blocks, (kept, given, product) = refs[:count], refs[-3:]
    half = product.shape[0] // 2
    for i, block in enumerate(blocks):
        product[...] = dot16(block[...], w_out[...], NN).astype(BF)
        rows = slice(i * half, (i + 1) * half)
        kept[rows, :] = product[pl.ds(pl.multiple_of(place[1] * half, half), half), :]
        given[rows, :] = product[pl.ds(pl.multiple_of((1 - place[1]) * half, half), half), :]


def output_part(place, w_out, blocks, before):
    vmem = pl.BlockSpec(memory_space=pltpu.VMEM)
    num_tok, columns = blocks[0].shape[0], w_out.shape[1]
    half = jax.ShapeDtypeStruct((len(blocks) * num_tok // 2, columns), BF)
    return pl.pallas_call(
        functools.partial(output_kernel, len(blocks)),
        out_shape=[half, half],
        in_specs=[pl.BlockSpec(memory_space=pltpu.SMEM)]
        + [vmem] * (1 + len(blocks))
        + [pl.BlockSpec(memory_space=pl.ANY)] * len(before),
        scratch_shapes=[pltpu.VMEM((num_tok, columns), BF)],
        compiler_params=PARAMS,
        cost_estimate=COST,
    )(place, w_out, *blocks, *before)


def core_kernel(count, half, place, kept, got, *refs):
    mine, *theirs, total = refs
    chips = 1 + len(theirs)
    share = half // chips
    total[...] = (kept[...].astype(F32) + got[...].astype(F32)).astype(BF)
    for turn, out in enumerate((mine, *theirs)):
        at = lax.rem(place[0] + turn, chips) * share
        for i in range(count):
            rows = pl.ds(pl.multiple_of(i * half + at, share), share)
            out[i * share : (i + 1) * share, :] = total[rows, :]


def core_part(place, kept, got, chips, half):
    vmem = pl.BlockSpec(memory_space=pltpu.VMEM)
    rows, columns = kept.shape
    share = jax.ShapeDtypeStruct((rows // chips, columns), BF)
    mine, *theirs = pl.pallas_call(
        functools.partial(core_kernel, rows // half, half),
        out_shape=[share] * chips,
        in_specs=[pl.BlockSpec(memory_space=pltpu.SMEM), vmem, vmem],
        scratch_shapes=[pltpu.VMEM((rows, columns), BF)],
        compiler_params=PARAMS,
        cost_estimate=COST,
    )(place, kept, got)
    return mine, theirs


def chip_kernel(count, others, mine, *refs):
    theirs, outs = refs[:others], refs[-count:]
    share = mine.shape[0] // count
    for i, out in enumerate(outs):
        rows = slice(i * share, (i + 1) * share)
        total = mine[rows, :].astype(F32)
        for block in theirs:
            total += block[rows, :].astype(F32)
        out[...] = total.astype(BF)


def chip_part(mine, theirs, count, before):
    rows, columns = mine.shape
    vmem = pl.BlockSpec(memory_space=pltpu.VMEM)
    return pl.pallas_call(
        functools.partial(chip_kernel, count, len(theirs)),
        out_shape=[jax.ShapeDtypeStruct((rows // count, columns), BF)] * count,
        in_specs=[vmem] * (1 + len(theirs)) + [pl.BlockSpec(memory_space=pl.ANY)] * len(before),
        compiler_params=PARAMS,
        cost_estimate=COST,
    )(mine, *theirs, *before)


def hold_kernel(count, *refs):
    for source, out in zip(refs[:count], refs[-count:]):
        out[...] = source[...]


def hold_part(arrays, before):
    vmem = pl.BlockSpec(memory_space=pltpu.VMEM)
    return pl.pallas_call(
        functools.partial(hold_kernel, len(arrays)),
        out_shape=[jax.ShapeDtypeStruct(x.shape, x.dtype) for x in arrays],
        in_specs=[vmem] * len(arrays) + [pl.BlockSpec(memory_space=pl.ANY)] * len(before),
        compiler_params=PARAMS,
        cost_estimate=COST,
    )(*arrays, *before)


def order_kernel(count, place, *refs):
    out = refs[-1]
    rows = refs[0].shape[0]
    for k in range(count):
        source = lax.rem(place[4] - k + count, count)
        at = (lax.rem(source, 2) * (count // 2) + lax.div(source, 2)) * rows
        out[pl.ds(pl.multiple_of(at, rows), rows), :] = refs[k][...]


def order_part(place, shares):
    vmem = pl.BlockSpec(memory_space=pltpu.VMEM)
    rows, columns = shares[0].shape
    return pl.pallas_call(
        functools.partial(order_kernel, len(shares)),
        out_shape=jax.ShapeDtypeStruct((rows * len(shares), columns), BF),
        in_specs=[pl.BlockSpec(memory_space=pltpu.SMEM)] + [vmem] * len(shares),
        compiler_params=PARAMS,
        cost_estimate=COST,
    )(place, *shares)


def body(
    tokens,
    w_x,
    w_bc,
    w_dt,
    dt_bias,
    decay_rate,
    skip_gain,
    w_out,
    suffix_lengths,
    checkpoint_slot,
    cache,
):
    reqs = lax.axis_size("req")
    tensors = lax.axis_size("tensor")
    chips = tensors // 2
    own_req = lax.axis_index("req")
    own_tensor = lax.axis_index("tensor")
    own_chip = own_tensor // 2
    core = own_tensor % 2
    num_tok = tokens.shape[0]
    depth = w_x.shape[0]
    slots_dev, heads, width, state_dim = cache.shape
    columns = heads * width
    half = depth // 2
    piece = num_tok // chips
    piece = num_tok // chips

    places = jnp.arange(num_tok, dtype=jnp.int32)
    ends = jnp.cumsum(suffix_lengths[0])
    seg = jnp.sum((places[:, None] >= ends[None, :]).astype(jnp.int32), axis=1)

    share = w_bc.shape[1] // tensors
    bc_share = lax.dynamic_slice_in_dim(w_bc, own_tensor * share, share, axis=1)
    w_small = jnp.concatenate(
        [bc_share, w_dt, w_dt, jnp.zeros((depth, LANES - share - 2 * heads), BF)], axis=1
    )
    place = jnp.stack(
        [own_chip, core, 0 * core + share + heads, 0 * core + share + 2 * heads, own_tensor]
    ).astype(jnp.int32)
    own_block = lax.dynamic_slice(tokens, (0, own_req * depth), (num_tok, depth))
    parts = [jnp.dot(own_block, w_x, preferred_element_type=F32).astype(BF)]
    smalls = [jnp.dot(own_block, w_small, preferred_element_type=F32)]
    order = sorted(range(1, reqs), key=lambda k: min(k, reqs - k))
    def token_block(k, first, rows):
        start = ((own_req + k) % reqs) * depth + core * half
        return lax.dynamic_slice(tokens, (first, start), (rows, half))

    arrived = [turn_req(token_block(k, 0, num_tok), k) for k in order[:-1]]
    products = []
    for k, near in zip(order, arrived):
        block, small = block_part(place, w_small, [near], [swap_core(near)], [])
        smalls.append(turn_req(small, -k))
        products.append(product_part(block, w_x, []))
        parts.append(turn_req(products[-1], -k))
    (near,) = hold_part([token_block(order[-1], own_chip * piece, piece)], arrived[-1:])
    near = turn_req(near, order[-1])
    near = [near] + [turn_chip(near, turn) for turn in range(1, chips)]
    far = [swap_core(block) for block in near]
    block, small = block_part(place, w_small, near, far, smalls[1:] + parts[1:2])
    smalls.append(turn_req(small, -order[-1]))
    products.append(product_part(block, w_x, smalls[-1:]))
    parts.append(turn_req(products[-1], -order[-1]))

    bc_share, raw_t = fold_part(smalls[0], smalls[1:], share, heads, [*parts[1:-1], products[-1]])
    quarters = [bc_share] + [turn_tensor(bc_share, k) for k in range(1, tensors)]
    bc_t, c_seg, tail_t, run, run_t, step_t = prep(
        place, raw_t, dt_bias, decay_rate, seg, quarters, []
    )
    c_segs = [c_seg] + [turn_req(c_seg, k) for k in range(1, reqs)]
    x, bundle = gather_part(parts, bc_t, tail_t, [])
    below, above = line_gather(bundle)

    per_pair = (slots_dev + reqs - 1) // reqs
    total_reqs = checkpoint_slot.shape[0]
    req_dev = total_reqs // reqs
    holder = checkpoint_slot // slots_dev
    index = jnp.arange(total_reqs, dtype=jnp.int32)
    owner = index // req_dev
    pair_key = holder * reqs + owner
    rank_in_pair = jnp.sum(
        (pair_key[:, None] == pair_key[None, :])
        & (checkpoint_slot[None, :] < checkpoint_slot[:, None]),
        axis=1,
    )
    away = (own_req - owner) % reqs
    pairs = jnp.arange(reqs * per_pair, dtype=jnp.int32)
    match = (holder == own_req)[None, :] & (
        (away * per_pair + rank_in_pair)[None, :] == pairs[:, None]
    )

    def pick(match, values, missing):
        found = jnp.sum(jnp.where(match, values[None, :], 0), axis=1)
        return jnp.where(jnp.any(match, axis=1), found, missing).astype(jnp.int32)

    pair_slot = pick(match, checkpoint_slot % slots_dev, 0)
    pair_member = pick(match, index % req_dev, -1)

    carried = carried_part(pair_slot, pair_member, c_segs, cache, [])

    base, grown = within_part(x, bc_t, seg, run, run_t, step_t, skip_gain)
    outputs = outputs_part(base, grown, line_sum(carried), [below[-1], above[-1]])

    slot_ids = own_req * slots_dev + jnp.arange(slots_dev, dtype=jnp.int32)
    match_slot = checkpoint_slot[None, :] == slot_ids[:, None]
    which = jnp.where(owner <= own_req, own_req - owner, reqs - 1 + owner - own_req)

    def sum_cores(kept, given):
        mine, theirs = core_part(place, kept, swap_core(given), chips, num_tok // 2)
        return mine, [turn_chip(block, turn + 1) for turn, block in enumerate(theirs)]

    far = order[-1]
    came = {k: turn_req(outputs, k) for k in order}
    kept, given = output_part(place, w_out, [outputs, came[far]], [below[-1],above[-1]])
    new_cache, zero = states_part(
        pick(match_slot, which, -1),
        pick(match_slot, index % req_dev, -1),
        cache,
        [bundle, *below, *above],
        [kept],
    )
    arrived = {}
    arrived[0], block = chip_part(*sum_cores(kept, given), 2, [])
    arrived[far] = turn_req(block, -far)
    before = [zero, block]
    for k in order[:-1]:
        kept, given = output_part(place, w_out, [came[k]], before)
        returned = [arrived[j] for j in order if j in arrived] if k == order[-2] else []
        (block,) = chip_part(*sum_cores(kept, given), 1, returned)
        arrived[k] = turn_req(block, -k)
        before = [block]

    def column_block(req):
        chosen = arrived[0]
        for k in range(1, reqs):
            chosen = jnp.where((req - own_req) % reqs == k, arrived[k], chosen)
        return chosen

    shares = [column_block(own_tensor)]
    for k in range(1, tensors):
        block = column_block((own_tensor + k) % tensors)
        shares.append(
            lax.ppermute(block, "tensor", [(i, (i + k) % tensors) for i in range(tensors)])
        )
    layer_out = order_part(place, shares)
    return (layer_out, new_cache)


def solution(mesh):
    placed = (
        P(("groups", "req"), None),
        P("req", "tensor"),
        P("req", None),
        P("req", "tensor"),
        P("tensor"),
        P("tensor"),
        P("tensor"),
        P("tensor", "req"),
        P(("groups", "req"), None),
        P("groups"),
        P(("groups", "req"), "tensor", None, None),
    )
    return jax.shard_map(
        body,
        mesh=mesh,
        in_specs=placed,
        out_specs=(P(("groups", "req"), "tensor"), P(("groups", "req"), "tensor", None, None)),
        check_vma=False,
    )
```

```python
import functools

import jax
import jax.numpy as jnp
from jax import lax
from jax.experimental import pallas as pl
from jax.experimental.pallas import tpu as pltpu
from jax.sharding import PartitionSpec as P

HIGH = lax.Precision.HIGHEST
BF = jnp.bfloat16
F32 = jnp.float32
NN = (((1,), (0,)), ((), ()))
NT = (((1,), (1,)), ((), ()))
TN = (((0,), (0,)), ((), ()))
TT = (((0,), (1,)), ((), ()))
LANES = 128
PARAMS = pltpu.CompilerParams(vmem_limit_bytes=24 * 1024 * 1024)
COST = pl.CostEstimate(flops=1, bytes_accessed=1, transcendentals=0)


def turn_req(x, turn):
    count = lax.axis_size("req")
    return lax.ppermute(x, "req", [(i, (i + turn) % count) for i in range(count)])


def step_up(x, first, last):
    return lax.ppermute(x, "req", [(i, i + 1) for i in range(first, last)])


def step_down(x, first, last):
    top = lax.axis_size("req") - 1
    return lax.ppermute(x, "req", [(top - i, top - i - 1) for i in range(first, last)])


def line_gather(x):
    count = lax.axis_size("req")
    below, above = [], []
    low = high = x
    for hop in range(count - 1):
        low, high = step_up(low, hop, count - 1), step_down(high, hop, count - 1)
        below.append(low)
        above.append(high)
    return below, above


def line_sum(blocks):
    count = lax.axis_size("req")
    low, high = blocks[1], blocks[count - 1]
    for hop in range(1, count):
        if hop > 1:
            low, high = low + blocks[hop], high + blocks[count - hop]
        low, high = step_up(low, 0, hop), step_down(high, 0, hop)
    return blocks[0], low, high


def swap_core(x):
    count = lax.axis_size("tensor")
    return lax.ppermute(x, "tensor", [(i, i ^ 1) for i in range(count)])


def turn_chip(x, turn):
    count = lax.axis_size("tensor")
    return lax.ppermute(x, "tensor", [(i, (i + 2 * turn) % count) for i in range(count)])


def turn_tensor(x, turn):
    count = lax.axis_size("tensor")
    return lax.ppermute(x, "tensor", [(i, (i + turn) % count) for i in range(count)])


def dot32(a, b, dims):
    return lax.dot_general(a, b, dims, precision=HIGH, preferred_element_type=F32)


def dot16(a, b, dims):
    return lax.dot_general(a, b, dims, preferred_element_type=F32)


def block_kernel(chips, place, w_small, *refs):
    near, far, (block, small) = refs[:chips], refs[chips : 2 * chips], refs[-2:]
    piece, half = near[0].shape

    def fill(core):
        own, other = slice(core * half, (core + 1) * half), slice((1 - core) * half, (2 - core) * half)
        for i in range(chips):
            at = lax.rem(place[0] - i + chips, chips) * piece
            rows = pl.ds(pl.multiple_of(at, piece), piece)
            block[rows, own] = near[i][...]
            block[rows, other] = far[i][...]

    for core in range(2):
        pl.when(place[1] == core)(functools.partial(fill, core))
    sums = dot16(block[...], w_small[...], NN)
    lane = lax.broadcasted_iota(jnp.int32, sums.shape, 1)
    low = (lane >= place[2]) & (lane < place[3])
    high = sums.astype(BF)
    small[...] = jnp.where(low, sums - high.astype(F32), sums).astype(BF)


def block_part(place, w_small, near, far, before):
    chips = len(near)
    num_tok = near[0].shape[0] * chips
    vmem = pl.BlockSpec(memory_space=pltpu.VMEM)
    return pl.pallas_call(
        functools.partial(block_kernel, chips),
        out_shape=[
            jax.ShapeDtypeStruct((num_tok, w_small.shape[0]), BF),
            jax.ShapeDtypeStruct((num_tok, LANES), BF),
        ],
        in_specs=[pl.BlockSpec(memory_space=pltpu.SMEM)]
        + [vmem] * (1 + 2 * chips)
        + [pl.BlockSpec(memory_space=pl.ANY)] * len(before),
        compiler_params=PARAMS,
        cost_estimate=COST,
    )(place, w_small, *near, *far, *before)


def product_kernel(block, weights, *refs):
    refs[-1][...] = dot16(block[...], weights[...], NN).astype(BF)


def product_part(block, weights, before):
    vmem = pl.BlockSpec(memory_space=pltpu.VMEM)
    return pl.pallas_call(
        product_kernel,
        out_shape=jax.ShapeDtypeStruct((block.shape[0], weights.shape[1]), BF),
        in_specs=[vmem, vmem] + [pl.BlockSpec(memory_space=pl.ANY)] * len(before),
        compiler_params=PARAMS,
        cost_estimate=COST,
    )(block, weights, *before)


def fold_kernel(share, heads, count, own, *refs):
    parts, (bc_t, raw_t) = refs[:count], refs[-2:]
    lane = lax.broadcasted_iota(jnp.int32, own.shape, 1)
    total = jnp.where(lane < share + heads, own[...], 0.0)
    for part in parts:
        total += part[...].astype(F32)
    total = total.T
    bc_t[...] = total[:share].astype(BF)
    raw_t[...] = total[share : share + heads] + total[share + heads : share + 2 * heads]


def fold_part(own, parts, share, heads, before):
    num_tok = own.shape[0]
    vmem = pl.BlockSpec(memory_space=pltpu.VMEM)
    rest = pl.BlockSpec(memory_space=pl.ANY)
    return pl.pallas_call(
        functools.partial(fold_kernel, share, heads, len(parts)),
        out_shape=[
            jax.ShapeDtypeStruct((share, num_tok), BF),
            jax.ShapeDtypeStruct((heads, num_tok), F32),
        ],
        in_specs=[vmem] * (1 + len(parts)) + [rest] * len(before),
        compiler_params=PARAMS,
        cost_estimate=COST,
    )(own, *parts, *before)


def prep_kernel(count, place, raw_t, bias, rate, seg_row, seg_col, *refs):
    quarters, (bc_t, c_seg, tail_t, run, run_t, step_t) = refs[:count], refs[-6:]
    heads, num_tok = raw_t.shape
    share = quarters[0].shape[0]
    dim = bc_t.shape[0] // 2
    for k, quarter in enumerate(quarters):
        at = lax.rem(place[4] - k + count, count) * share
        bc_t[pl.ds(pl.multiple_of(at, share), share), :] = quarter[...]
    z = raw_t[...] + bias[...]
    step = jnp.maximum(z, 0.0) + jnp.log1p(jnp.exp(-jnp.abs(z)))
    log_decay = -step * rate[...]
    down = lax.broadcasted_iota(jnp.int32, (num_tok, num_tok), 0)
    along = lax.broadcasted_iota(jnp.int32, (num_tok, num_tok), 1)
    same = seg_row[...] == seg_col[...]
    causal = (same & (down >= along)).astype(F32)
    run[...] = dot32(causal, log_decay, NT)
    running = dot32(log_decay, causal, NT)
    totals = dot32(log_decay, same.astype(F32), NT)
    run_t[...] = running
    step_t[...] = step
    grown = jnp.exp(totals)
    high = grown.astype(BF)
    tail_t[...] = jnp.zeros_like(tail_t)
    tail_t[:heads, :] = (jnp.exp(jnp.minimum(totals - running, 0.0)) * step).astype(BF)
    tail_t[16 : 16 + heads, :] = high
    tail_t[32 : 32 + heads, :] = (grown - high.astype(F32)).astype(BF)
    seg_rows = jnp.broadcast_to(seg_col[...].astype(F32), (16, num_tok)).astype(BF)
    tail_t[48:64, :] = seg_rows
    c_seg[:dim, :] = bc_t[dim:, :]
    c_seg[dim:, :] = seg_rows


def prep(place, raw_t, bias, rate, seg, quarters, before):
    heads, num_tok = raw_t.shape
    rows = quarters[0].shape[0] * len(quarters)
    vmem = pl.BlockSpec(memory_space=pltpu.VMEM)
    return pl.pallas_call(
        functools.partial(prep_kernel, len(quarters)),
        out_shape=[
            jax.ShapeDtypeStruct((rows, num_tok), BF),
            jax.ShapeDtypeStruct((rows // 2 + 16, num_tok), BF),
            jax.ShapeDtypeStruct((64, num_tok), BF),
            jax.ShapeDtypeStruct((num_tok, heads), F32),
            jax.ShapeDtypeStruct((heads, num_tok), F32),
            jax.ShapeDtypeStruct((heads, num_tok), F32),
        ],
        in_specs=[pl.BlockSpec(memory_space=pltpu.SMEM)]
        + [vmem] * (5 + len(quarters))
        + [pl.BlockSpec(memory_space=pl.ANY)] * len(before),
        compiler_params=PARAMS,
        cost_estimate=COST,
    )(place, raw_t, bias[:, None], rate[:, None], seg[:, None], seg[None, :], *quarters, *before)


def carried_kernel(owners, ranks, slot, member, *refs):
    c_segs, outs = refs[:owners], refs[-owners:]
    states = refs[owners : owners + ranks]
    heads, width, dim = states[0].shape[1:]
    at = pl.program_id(0)
    flat = [state[0].reshape(heads * width, dim).astype(BF) for state in states]

    def fill(c_seg, out):
        c_rows = c_seg[:dim, :].astype(F32)
        seg = c_seg[dim : dim + 1, :].astype(F32)
        total = jnp.zeros(out.shape, F32)
        for rank in range(ranks):
            inside = seg == member[at * ranks + rank].astype(F32)
            mine = jnp.where(inside, c_rows, 0.0).T.astype(BF)
            total += dot16(mine, flat[rank], NT)
        out[...] = total.astype(BF)

    for i in range(owners):
        pl.when(at == i)(functools.partial(fill, c_segs[i], outs[i]))


def carried_part(slot, member, c_segs, cache, before):
    num_tok = c_segs[0].shape[1]
    _, heads, width, dim = cache.shape
    owners = len(c_segs)
    ranks = slot.shape[0] // owners

    def state_map(rank, i, slot, member):
        return (slot[i * ranks + rank], 0, 0, 0)

    return pl.pallas_call(
        functools.partial(carried_kernel, owners, ranks),
        out_shape=[jax.ShapeDtypeStruct((num_tok, heads * width), BF)] * owners,
        grid_spec=pltpu.PrefetchScalarGridSpec(
            num_scalar_prefetch=2,
            grid=(owners,),
            in_specs=[pl.BlockSpec(c_seg.shape, lambda i, *_: (0, 0)) for c_seg in c_segs]
            + [
                pl.BlockSpec((1, heads, width, dim), functools.partial(state_map, rank))
                for rank in range(ranks)
            ]
            + [pl.BlockSpec(memory_space=pl.ANY)] * len(before),
            out_specs=[pl.BlockSpec((num_tok, heads * width), lambda i, *_: (0, 0))] * owners,
        ),
        compiler_params=PARAMS,
        cost_estimate=COST,
    )(slot, member, *c_segs, *([cache] * ranks), *before)


def gather_kernel(count, *refs):
    parts = refs[:count]
    bc_t, tail_t = refs[count : count + 2]
    x, bundle = refs[-2:]
    columns = x.shape[1]
    dim = bc_t.shape[0] // 2
    for first in range(0, columns, LANES):
        at = slice(first, first + LANES)
        total = parts[0][:, at].astype(F32)
        for part in parts[1:]:
            total += part[:, at].astype(F32)
        x[:, at] = total.astype(BF)
        bundle[at, :] = total.T.astype(BF)
    bundle[columns : columns + dim, :] = bc_t[:dim, :]
    bundle[columns + dim :, :] = tail_t[...]


def gather_part(parts, bc_t, tail_t, before):
    num_tok, columns = parts[0].shape
    rows = columns + bc_t.shape[0] // 2 + tail_t.shape[0]
    vmem = pl.BlockSpec(memory_space=pltpu.VMEM)
    return pl.pallas_call(
        functools.partial(gather_kernel, len(parts)),
        out_shape=[
            jax.ShapeDtypeStruct((num_tok, columns), BF),
            jax.ShapeDtypeStruct((rows, num_tok), BF),
        ],
        in_specs=[vmem] * (len(parts) + 2) + [pl.BlockSpec(memory_space=pl.ANY)] * len(before),
        compiler_params=PARAMS,
        cost_estimate=COST,
    )(*parts, bc_t, tail_t, *before)


def within_kernel(x, bc_t, seg_row, seg_col, run, run_t, step_t, gain, base, grown):
    num_tok, columns = base.shape
    heads = run.shape[1]
    width = columns // heads
    down = lax.broadcasted_iota(jnp.int32, (num_tok, num_tok), 0)
    along = lax.broadcasted_iota(jnp.int32, (num_tok, num_tok), 1)
    keep = (seg_row[...] == seg_col[...]) & (down >= along)
    dim = bc_t.shape[0] // 2
    raw = dot16(bc_t[dim:, :], bc_t[:dim, :], TN)
    scores = jnp.where(keep, raw, 0.0)
    pair = LANES // width
    lane = lax.broadcasted_iota(jnp.int32, (num_tok, LANES), 1) // width
    for first in range(0, heads, pair):
        at = slice(first * width, (first + pair) * width)
        values = x[:, at]
        exact = values.astype(F32)
        total = jnp.zeros((num_tok, LANES), F32)
        rise = jnp.zeros((num_tok, LANES), F32)
        for i in range(pair):
            h = first + i
            run_col = run[:, h : h + 1]
            decay = jnp.exp(jnp.minimum(run_col - run_t[h : h + 1, :], 0.0))
            mixing = (decay * scores * step_t[h : h + 1, :]).astype(BF)
            inner = dot16(mixing, values, NN) + gain[:, h : h + 1] * exact
            total = jnp.where(lane == i, inner, total)
            rise = jnp.where(lane == i, jnp.exp(run_col), rise)
        base[:, at] = total
        grown[:, at] = rise


def within_part(x, bc_t, seg, run, run_t, step_t, gain):
    num_tok, columns = x.shape
    heads = run.shape[1]
    return pl.pallas_call(
        within_kernel,
        out_shape=[jax.ShapeDtypeStruct((num_tok, columns), F32)] * 2,
        compiler_params=PARAMS,
        cost_estimate=COST,
    )(x, bc_t, seg[:, None], seg[None, :], run, run_t, step_t, gain[None])


def outputs_kernel(count, base, grown, *refs):
    held = refs[0][...].astype(F32)
    for block in refs[1:count]:
        held += block[...].astype(F32)
    refs[-1][...] = (base[...] + grown[...] * held).astype(BF)


def outputs_part(base, grown, carried, before):
    vmem = pl.BlockSpec(memory_space=pltpu.VMEM)
    rest = pl.BlockSpec(memory_space=pl.ANY)
    return pl.pallas_call(
        functools.partial(outputs_kernel, len(carried)),
        out_shape=jax.ShapeDtypeStruct(base.shape, BF),
        in_specs=[vmem] * (2 + len(carried)) + [rest] * len(before),
        compiler_params=PARAMS,
        cost_estimate=COST,
    )(base, grown, *carried, *before)


def states_kernel(sources, which, member, state, *refs):
    bundles, (out, done) = refs[:sources], refs[-2:]
    heads, width, dim = state.shape[1:]
    columns = heads * width
    at = pl.program_id(0)
    done[...] = jnp.zeros_like(done)

    def update(bundle):
        b_rows = bundle[columns : columns + dim, :]
        tail = bundle[columns + dim :, :].astype(F32)
        inside = tail[48:49] == member[at].astype(F32)
        weights = jnp.where(inside, tail[:heads], 0.0)
        rise = tail[16 : 16 + heads] + tail[32 : 32 + heads]
        rise = jnp.max(jnp.where(inside, rise, 0.0), axis=1, keepdims=True)
        for h in range(heads):
            rows = slice(h * width, (h + 1) * width)
            scaled = (bundle[rows, :].astype(F32) * weights[h : h + 1]).astype(BF)
            out[0, h] = state[0, h] * rise[h : h + 1] + dot16(scaled, b_rows, NT)

    for i in range(sources):
        pl.when(which[at] == i)(functools.partial(update, bundles[i]))

    @pl.when(which[at] < 0)
    def _():
        out[...] = state[...]


def states_part(which, member, cache, bundles, before):
    slots, heads, width, dim = cache.shape
    rows, num_tok = bundles[0].shape
    slab = pl.BlockSpec((1, heads, width, dim), lambda s, *_: (s, 0, 0, 0))
    fixed = pl.BlockSpec((rows, num_tok), lambda s, *_: (0, 0))
    return pl.pallas_call(
        functools.partial(states_kernel, len(bundles)),
        out_shape=[
            jax.ShapeDtypeStruct(cache.shape, cache.dtype),
            jax.ShapeDtypeStruct((8, LANES), jnp.int32),
        ],
        grid_spec=pltpu.PrefetchScalarGridSpec(
            num_scalar_prefetch=2,
            grid=(slots,),
            in_specs=[slab]
            + [fixed] * len(bundles)
            + [pl.BlockSpec(memory_space=pl.ANY)] * len(before),
            out_specs=[slab, pl.BlockSpec((8, LANES), lambda s, *_: (0, 0))],
        ),
        compiler_params=PARAMS,
        cost_estimate=COST,
    )(which, member, cache, *bundles, *before)


def output_kernel(count, place, w_out, *refs):
    blocks, (kept, given, product) = refs[:count], refs[-3:]
    half = product.shape[0] // 2
    for i, block in enumerate(blocks):
        product[...] = dot16(block[...], w_out[...], NN).astype(BF)
        rows = slice(i * half, (i + 1) * half)
        kept[rows, :] = product[pl.ds(pl.multiple_of(place[1] * half, half), half), :]
        given[rows, :] = product[pl.ds(pl.multiple_of((1 - place[1]) * half, half), half), :]


def output_part(place, w_out, blocks, before):
    vmem = pl.BlockSpec(memory_space=pltpu.VMEM)
    num_tok, columns = blocks[0].shape[0], w_out.shape[1]
    half = jax.ShapeDtypeStruct((len(blocks) * num_tok // 2, columns), BF)
    return pl.pallas_call(
        functools.partial(output_kernel, len(blocks)),
        out_shape=[half, half],
        in_specs=[pl.BlockSpec(memory_space=pltpu.SMEM)]
        + [vmem] * (1 + len(blocks))
        + [pl.BlockSpec(memory_space=pl.ANY)] * len(before),
        scratch_shapes=[pltpu.VMEM((num_tok, columns), BF)],
        compiler_params=PARAMS,
        cost_estimate=COST,
    )(place, w_out, *blocks, *before)


def core_kernel(count, half, place, kept, got, *refs):
    mine, *theirs, total = refs
    chips = 1 + len(theirs)
    share = half // chips
    total[...] = (kept[...].astype(F32) + got[...].astype(F32)).astype(BF)
    for turn, out in enumerate((mine, *theirs)):
        at = lax.rem(place[0] + turn, chips) * share
        for i in range(count):
            rows = pl.ds(pl.multiple_of(i * half + at, share), share)
            out[i * share : (i + 1) * share, :] = total[rows, :]


def core_part(place, kept, got, chips, half):
    vmem = pl.BlockSpec(memory_space=pltpu.VMEM)
    rows, columns = kept.shape
    share = jax.ShapeDtypeStruct((rows // chips, columns), BF)
    mine, *theirs = pl.pallas_call(
        functools.partial(core_kernel, rows // half, half),
        out_shape=[share] * chips,
        in_specs=[pl.BlockSpec(memory_space=pltpu.SMEM), vmem, vmem],
        scratch_shapes=[pltpu.VMEM((rows, columns), BF)],
        compiler_params=PARAMS,
        cost_estimate=COST,
    )(place, kept, got)
    return mine, theirs


def chip_kernel(count, others, mine, *refs):
    theirs, outs = refs[:others], refs[-count:]
    share = mine.shape[0] // count
    for i, out in enumerate(outs):
        rows = slice(i * share, (i + 1) * share)
        total = mine[rows, :].astype(F32)
        for block in theirs:
            total += block[rows, :].astype(F32)
        out[...] = total.astype(BF)


def chip_part(mine, theirs, count, before):
    rows, columns = mine.shape
    vmem = pl.BlockSpec(memory_space=pltpu.VMEM)
    return pl.pallas_call(
        functools.partial(chip_kernel, count, len(theirs)),
        out_shape=[jax.ShapeDtypeStruct((rows // count, columns), BF)] * count,
        in_specs=[vmem] * (1 + len(theirs)) + [pl.BlockSpec(memory_space=pl.ANY)] * len(before),
        compiler_params=PARAMS,
        cost_estimate=COST,
    )(mine, *theirs, *before)


def hold_kernel(count, *refs):
    for source, out in zip(refs[:count], refs[-count:]):
        out[...] = source[...]


def hold_part(arrays, before):
    vmem = pl.BlockSpec(memory_space=pltpu.VMEM)
    return pl.pallas_call(
        functools.partial(hold_kernel, len(arrays)),
        out_shape=[jax.ShapeDtypeStruct(x.shape, x.dtype) for x in arrays],
        in_specs=[vmem] * len(arrays) + [pl.BlockSpec(memory_space=pl.ANY)] * len(before),
        compiler_params=PARAMS,
        cost_estimate=COST,
    )(*arrays, *before)


def order_kernel(count, place, *refs):
    out = refs[-1]
    rows = refs[0].shape[0]
    for k in range(count):
        source = lax.rem(place[4] - k + count, count)
        at = (lax.rem(source, 2) * (count // 2) + lax.div(source, 2)) * rows
        out[pl.ds(pl.multiple_of(at, rows), rows), :] = refs[k][...]


def order_part(place, shares):
    vmem = pl.BlockSpec(memory_space=pltpu.VMEM)
    rows, columns = shares[0].shape
    return pl.pallas_call(
        functools.partial(order_kernel, len(shares)),
        out_shape=jax.ShapeDtypeStruct((rows * len(shares), columns), BF),
        in_specs=[pl.BlockSpec(memory_space=pltpu.SMEM)] + [vmem] * len(shares),
        compiler_params=PARAMS,
        cost_estimate=COST,
    )(place, *shares)


def body(
    tokens,
    w_x,
    w_bc,
    w_dt,
    dt_bias,
    decay_rate,
    skip_gain,
    w_out,
    suffix_lengths,
    checkpoint_slot,
    cache,
):
    reqs = lax.axis_size("req")
    tensors = lax.axis_size("tensor")
    chips = tensors // 2
    own_req = lax.axis_index("req")
    own_tensor = lax.axis_index("tensor")
    own_chip = own_tensor // 2
    core = own_tensor % 2
    num_tok = tokens.shape[0]
    depth = w_x.shape[0]
    slots_dev, heads, width, state_dim = cache.shape
    columns = heads * width
    half = depth // 2
    piece = num_tok // chips
    piece = num_tok // chips

    places = jnp.arange(num_tok, dtype=jnp.int32)
    ends = jnp.cumsum(suffix_lengths[0])
    seg = jnp.sum((places[:, None] >= ends[None, :]).astype(jnp.int32), axis=1)

    share = w_bc.shape[1] // tensors
    bc_share = lax.dynamic_slice_in_dim(w_bc, own_tensor * share, share, axis=1)
    w_small = jnp.concatenate(
        [bc_share, w_dt, w_dt, jnp.zeros((depth, LANES - share - 2 * heads), BF)], axis=1
    )
    place = jnp.stack(
        [own_chip, core, 0 * core + share + heads, 0 * core + share + 2 * heads, own_tensor]
    ).astype(jnp.int32)
    own_block = lax.dynamic_slice(tokens, (0, own_req * depth), (num_tok, depth))
    parts = [jnp.dot(own_block, w_x, preferred_element_type=F32).astype(BF)]
    smalls = [jnp.dot(own_block, w_small, preferred_element_type=F32)]
    order = sorted(range(1, reqs), key=lambda k: min(k, reqs - k))
    def token_block(k, first, rows):
        start = ((own_req + k) % reqs) * depth + core * half
        return lax.dynamic_slice(tokens, (first, start), (rows, half))

    arrived = [token_block(k, 0, num_tok) for k in order[:-1]]
    for i in range(1, len(arrived)):
        (arrived[i],) = hold_part(arrived[i : i + 1], [arrived[i - 1]])
    arrived = [turn_req(block, k) for k, block in zip(order, arrived)]
    blocks = []
    for i, (k, near) in enumerate(zip(order, arrived)):
        block, small = block_part(place, w_small, [near], [swap_core(near)], [])
        smalls.append(turn_req(small, -k))
        blocks.append(block)
        if i == 0:
            products = [product_part(block, w_x, [])]
            parts.append(turn_req(products[0], -k))
    near = turn_req(token_block(order[-1], own_chip * piece, piece), order[-1])
    near = [near] + [turn_chip(near, turn) for turn in range(1, chips)]
    far = [swap_core(block) for block in near]
    block, small = block_part(place, w_small, near, far, smalls[1:] + parts[1:2])
    smalls.append(turn_req(small, -order[-1]))
    for k, near in zip(order[1:-1], blocks[1:]):
        products.append(product_part(near, w_x, [small]))
        parts.append(turn_req(products[-1], -k))
    products.append(product_part(block, w_x, smalls[-1:]))
    parts.append(turn_req(products[-1], -order[-1]))

    bc_share, raw_t = fold_part(smalls[0], smalls[1:], share, heads, [*parts[1:-1], products[-1]])
    quarters = [bc_share] + [turn_tensor(bc_share, k) for k in range(1, tensors)]
    bc_t, c_seg, tail_t, run, run_t, step_t = prep(
        place, raw_t, dt_bias, decay_rate, seg, quarters, []
    )
    c_segs = [c_seg] + [turn_req(c_seg, k) for k in range(1, reqs)]
    x, bundle = gather_part(parts, bc_t, tail_t, [])
    below, above = line_gather(bundle)

    per_pair = (slots_dev + reqs - 1) // reqs
    total_reqs = checkpoint_slot.shape[0]
    req_dev = total_reqs // reqs
    holder = checkpoint_slot // slots_dev
    index = jnp.arange(total_reqs, dtype=jnp.int32)
    owner = index // req_dev
    pair_key = holder * reqs + owner
    rank_in_pair = jnp.sum(
        (pair_key[:, None] == pair_key[None, :])
        & (checkpoint_slot[None, :] < checkpoint_slot[:, None]),
        axis=1,
    )
    away = (own_req - owner) % reqs
    pairs = jnp.arange(reqs * per_pair, dtype=jnp.int32)
    match = (holder == own_req)[None, :] & (
        (away * per_pair + rank_in_pair)[None, :] == pairs[:, None]
    )

    def pick(match, values, missing):
        found = jnp.sum(jnp.where(match, values[None, :], 0), axis=1)
        return jnp.where(jnp.any(match, axis=1), found, missing).astype(jnp.int32)

    pair_slot = pick(match, checkpoint_slot % slots_dev, 0)
    pair_member = pick(match, index % req_dev, -1)

    carried = carried_part(pair_slot, pair_member, c_segs, cache, [])

    base, grown = within_part(x, bc_t, seg, run, run_t, step_t, skip_gain)
    outputs = outputs_part(base, grown, line_sum(carried), [below[-1], above[-1]])

    slot_ids = own_req * slots_dev + jnp.arange(slots_dev, dtype=jnp.int32)
    match_slot = checkpoint_slot[None, :] == slot_ids[:, None]
    which = jnp.where(owner <= own_req, own_req - owner, reqs - 1 + owner - own_req)

    def sum_cores(kept, given):
        mine, theirs = core_part(place, kept, swap_core(given), chips, num_tok // 2)
        return mine, [turn_chip(block, turn + 1) for turn, block in enumerate(theirs)]

    far = order[-1]
    came = {k: turn_req(outputs, k) for k in order}
    kept, given = output_part(place, w_out, [outputs, came[far]], [below[-1], above[-1]])
    new_cache, zero = states_part(
        pick(match_slot, which, -1),
        pick(match_slot, index % req_dev, -1),
        cache,
        [bundle, *below, *above],
        [kept],
    )
    arrived = {}
    arrived[0], block = chip_part(*sum_cores(kept, given), 2, [])
    arrived[far] = turn_req(block, -far)
    before = [zero, block]
    for k in order[:-1]:
        kept, given = output_part(place, w_out, [came[k]], before)
        returned = [arrived[j] for j in order if j in arrived] if k == order[-2] else []
        (block,) = chip_part(*sum_cores(kept, given), 1, returned)
        arrived[k] = turn_req(block, -k)
        before = [block]

    def column_block(req):
        chosen = arrived[0]
        for k in range(1, reqs):
            chosen = jnp.where((req - own_req) % reqs == k, arrived[k], chosen)
        return chosen

    shares = [column_block(own_tensor)]
    for k in range(1, tensors):
        block = column_block((own_tensor + k) % tensors)
        shares.append(
            lax.ppermute(block, "tensor", [(i, (i + k) % tensors) for i in range(tensors)])
        )
    layer_out = order_part(place, shares)
    return (layer_out, new_cache)


def solution(mesh):
    placed = (
        P(("groups", "req"), None),
        P("req", "tensor"),
        P("req", None),
        P("req", "tensor"),
        P("tensor"),
        P("tensor"),
        P("tensor"),
        P("tensor", "req"),
        P(("groups", "req"), None),
        P("groups"),
        P(("groups", "req"), "tensor", None, None),
    )
    return jax.shard_map(
        body,
        mesh=mesh,
        in_specs=placed,
        out_specs=(P(("groups", "req"), "tensor"), P(("groups", "req"), "tensor", None, None)),
        check_vma=False,
    )
```

```python
import functools

import jax
import jax.numpy as jnp
from jax import lax
from jax.experimental import pallas as pl
from jax.experimental.pallas import tpu as pltpu
from jax.sharding import PartitionSpec as P

HIGH = lax.Precision.HIGHEST
BF = jnp.bfloat16
F32 = jnp.float32
NN = (((1,), (0,)), ((), ()))
NT = (((1,), (1,)), ((), ()))
TN = (((0,), (0,)), ((), ()))
TT = (((0,), (1,)), ((), ()))
LANES = 128
PARAMS = pltpu.CompilerParams(vmem_limit_bytes=24 * 1024 * 1024)
COST = pl.CostEstimate(flops=1, bytes_accessed=1, transcendentals=0)


def turn_req(x, turn):
    count = lax.axis_size("req")
    return lax.ppermute(x, "req", [(i, (i + turn) % count) for i in range(count)])


def step_up(x, first, last):
    return lax.ppermute(x, "req", [(i, i + 1) for i in range(first, last)])


def step_down(x, first, last):
    top = lax.axis_size("req") - 1
    return lax.ppermute(x, "req", [(top - i, top - i - 1) for i in range(first, last)])


def line_gather(x):
    count = lax.axis_size("req")
    below, above = [], []
    low = high = x
    for hop in range(count - 1):
        low, high = step_up(low, hop, count - 1), step_down(high, hop, count - 1)
        below.append(low)
        above.append(high)
    return below, above


def line_sum(blocks):
    count = lax.axis_size("req")
    low, high = blocks[1], blocks[count - 1]
    for hop in range(1, count):
        if hop > 1:
            low, high = low + blocks[hop], high + blocks[count - hop]
        low, high = step_up(low, 0, hop), step_down(high, 0, hop)
    return blocks[0], low, high


def swap_core(x):
    count = lax.axis_size("tensor")
    return lax.ppermute(x, "tensor", [(i, i ^ 1) for i in range(count)])


def turn_chip(x, turn):
    count = lax.axis_size("tensor")
    return lax.ppermute(x, "tensor", [(i, (i + 2 * turn) % count) for i in range(count)])


def turn_tensor(x, turn):
    count = lax.axis_size("tensor")
    return lax.ppermute(x, "tensor", [(i, (i + turn) % count) for i in range(count)])


def dot32(a, b, dims):
    return lax.dot_general(a, b, dims, precision=HIGH, preferred_element_type=F32)


def dot16(a, b, dims):
    return lax.dot_general(a, b, dims, preferred_element_type=F32)


def block_kernel(chips, place, w_small, *refs):
    near, far, (block, small) = refs[:chips], refs[chips : 2 * chips], refs[-2:]
    piece, half = near[0].shape

    def fill(core):
        own, other = slice(core * half, (core + 1) * half), slice((1 - core) * half, (2 - core) * half)
        for i in range(chips):
            at = lax.rem(place[0] - i + chips, chips) * piece
            rows = pl.ds(pl.multiple_of(at, piece), piece)
            block[rows, own] = near[i][...]
            block[rows, other] = far[i][...]

    for core in range(2):
        pl.when(place[1] == core)(functools.partial(fill, core))
    sums = dot16(block[...], w_small[...], NN)
    lane = lax.broadcasted_iota(jnp.int32, sums.shape, 1)
    low = (lane >= place[2]) & (lane < place[3])
    high = sums.astype(BF)
    small[...] = jnp.where(low, sums - high.astype(F32), sums).astype(BF)


def block_part(place, w_small, near, far, before):
    chips = len(near)
    num_tok = near[0].shape[0] * chips
    vmem = pl.BlockSpec(memory_space=pltpu.VMEM)
    return pl.pallas_call(
        functools.partial(block_kernel, chips),
        out_shape=[
            jax.ShapeDtypeStruct((num_tok, w_small.shape[0]), BF),
            jax.ShapeDtypeStruct((num_tok, LANES), BF),
        ],
        in_specs=[pl.BlockSpec(memory_space=pltpu.SMEM)]
        + [vmem] * (1 + 2 * chips)
        + [pl.BlockSpec(memory_space=pl.ANY)] * len(before),
        compiler_params=PARAMS,
        cost_estimate=COST,
    )(place, w_small, *near, *far, *before)


def product_kernel(block, weights, *refs):
    refs[-1][...] = dot16(block[...], weights[...], NN).astype(BF)


def product_part(block, weights, before):
    vmem = pl.BlockSpec(memory_space=pltpu.VMEM)
    return pl.pallas_call(
        product_kernel,
        out_shape=jax.ShapeDtypeStruct((block.shape[0], weights.shape[1]), BF),
        in_specs=[vmem, vmem] + [pl.BlockSpec(memory_space=pl.ANY)] * len(before),
        compiler_params=PARAMS,
        cost_estimate=COST,
    )(block, weights, *before)


def fold_kernel(share, heads, count, own, *refs):
    parts, (bc_t, raw_t) = refs[:count], refs[-2:]
    lane = lax.broadcasted_iota(jnp.int32, own.shape, 1)
    total = jnp.where(lane < share + heads, own[...], 0.0)
    for part in parts:
        total += part[...].astype(F32)
    total = total.T
    bc_t[...] = total[:share].astype(BF)
    raw_t[...] = total[share : share + heads] + total[share + heads : share + 2 * heads]


def fold_part(own, parts, share, heads, before):
    num_tok = own.shape[0]
    vmem = pl.BlockSpec(memory_space=pltpu.VMEM)
    rest = pl.BlockSpec(memory_space=pl.ANY)
    return pl.pallas_call(
        functools.partial(fold_kernel, share, heads, len(parts)),
        out_shape=[
            jax.ShapeDtypeStruct((share, num_tok), BF),
            jax.ShapeDtypeStruct((heads, num_tok), F32),
        ],
        in_specs=[vmem] * (1 + len(parts)) + [rest] * len(before),
        compiler_params=PARAMS,
        cost_estimate=COST,
    )(own, *parts, *before)


def prep_kernel(count, place, raw_t, bias, rate, seg_row, seg_col, *refs):
    quarters, (bc_t, c_seg, tail_t, run, run_t, step_t) = refs[:count], refs[-6:]
    heads, num_tok = raw_t.shape
    share = quarters[0].shape[0]
    dim = bc_t.shape[0] // 2
    for k, quarter in enumerate(quarters):
        at = lax.rem(place[4] - k + count, count) * share
        bc_t[pl.ds(pl.multiple_of(at, share), share), :] = quarter[...]
    z = raw_t[...] + bias[...]
    step = jnp.maximum(z, 0.0) + jnp.log1p(jnp.exp(-jnp.abs(z)))
    log_decay = -step * rate[...]
    down = lax.broadcasted_iota(jnp.int32, (num_tok, num_tok), 0)
    along = lax.broadcasted_iota(jnp.int32, (num_tok, num_tok), 1)
    same = seg_row[...] == seg_col[...]
    causal = (same & (down >= along)).astype(F32)
    run[...] = dot32(causal, log_decay, NT)
    running = dot32(log_decay, causal, NT)
    totals = dot32(log_decay, same.astype(F32), NT)
    run_t[...] = running
    step_t[...] = step
    grown = jnp.exp(totals)
    high = grown.astype(BF)
    tail_t[...] = jnp.zeros_like(tail_t)
    tail_t[:heads, :] = (jnp.exp(jnp.minimum(totals - running, 0.0)) * step).astype(BF)
    tail_t[16 : 16 + heads, :] = high
    tail_t[32 : 32 + heads, :] = (grown - high.astype(F32)).astype(BF)
    seg_rows = jnp.broadcast_to(seg_col[...].astype(F32), (16, num_tok)).astype(BF)
    tail_t[48:64, :] = seg_rows
    c_seg[:dim, :] = bc_t[dim:, :]
    c_seg[dim:, :] = seg_rows


def prep(place, raw_t, bias, rate, seg, quarters, before):
    heads, num_tok = raw_t.shape
    rows = quarters[0].shape[0] * len(quarters)
    vmem = pl.BlockSpec(memory_space=pltpu.VMEM)
    return pl.pallas_call(
        functools.partial(prep_kernel, len(quarters)),
        out_shape=[
            jax.ShapeDtypeStruct((rows, num_tok), BF),
            jax.ShapeDtypeStruct((rows // 2 + 16, num_tok), BF),
            jax.ShapeDtypeStruct((64, num_tok), BF),
            jax.ShapeDtypeStruct((num_tok, heads), F32),
            jax.ShapeDtypeStruct((heads, num_tok), F32),
            jax.ShapeDtypeStruct((heads, num_tok), F32),
        ],
        in_specs=[pl.BlockSpec(memory_space=pltpu.SMEM)]
        + [vmem] * (5 + len(quarters))
        + [pl.BlockSpec(memory_space=pl.ANY)] * len(before),
        compiler_params=PARAMS,
        cost_estimate=COST,
    )(place, raw_t, bias[:, None], rate[:, None], seg[:, None], seg[None, :], *quarters, *before)


def carried_kernel(owners, ranks, slot, member, *refs):
    c_segs, outs = refs[:owners], refs[-owners:]
    states = refs[owners : owners + ranks]
    heads, width, dim = states[0].shape[1:]
    at = pl.program_id(0)
    flat = [state[0].reshape(heads * width, dim).astype(BF) for state in states]

    def fill(c_seg, out):
        c_rows = c_seg[:dim, :].astype(F32)
        seg = c_seg[dim : dim + 1, :].astype(F32)
        total = jnp.zeros(out.shape, F32)
        for rank in range(ranks):
            inside = seg == member[at * ranks + rank].astype(F32)
            mine = jnp.where(inside, c_rows, 0.0).T.astype(BF)
            total += dot16(mine, flat[rank], NT)
        out[...] = total.astype(BF)

    for i in range(owners):
        pl.when(at == i)(functools.partial(fill, c_segs[i], outs[i]))


def carried_part(slot, member, c_segs, cache, before):
    num_tok = c_segs[0].shape[1]
    _, heads, width, dim = cache.shape
    owners = len(c_segs)
    ranks = slot.shape[0] // owners

    def state_map(rank, i, slot, member):
        return (slot[i * ranks + rank], 0, 0, 0)

    return pl.pallas_call(
        functools.partial(carried_kernel, owners, ranks),
        out_shape=[jax.ShapeDtypeStruct((num_tok, heads * width), BF)] * owners,
        grid_spec=pltpu.PrefetchScalarGridSpec(
            num_scalar_prefetch=2,
            grid=(owners,),
            in_specs=[pl.BlockSpec(c_seg.shape, lambda i, *_: (0, 0)) for c_seg in c_segs]
            + [
                pl.BlockSpec((1, heads, width, dim), functools.partial(state_map, rank))
                for rank in range(ranks)
            ]
            + [pl.BlockSpec(memory_space=pl.ANY)] * len(before),
            out_specs=[pl.BlockSpec((num_tok, heads * width), lambda i, *_: (0, 0))] * owners,
        ),
        compiler_params=PARAMS,
        cost_estimate=COST,
    )(slot, member, *c_segs, *([cache] * ranks), *before)


def gather_kernel(count, *refs):
    parts = refs[:count]
    bc_t, tail_t = refs[count : count + 2]
    x, bundle = refs[-2:]
    columns = x.shape[1]
    dim = bc_t.shape[0] // 2
    for first in range(0, columns, LANES):
        at = slice(first, first + LANES)
        total = parts[0][:, at].astype(F32)
        for part in parts[1:]:
            total += part[:, at].astype(F32)
        x[:, at] = total.astype(BF)
        bundle[at, :] = total.T.astype(BF)
    bundle[columns : columns + dim, :] = bc_t[:dim, :]
    bundle[columns + dim :, :] = tail_t[...]


def gather_part(parts, bc_t, tail_t, before):
    num_tok, columns = parts[0].shape
    rows = columns + bc_t.shape[0] // 2 + tail_t.shape[0]
    vmem = pl.BlockSpec(memory_space=pltpu.VMEM)
    return pl.pallas_call(
        functools.partial(gather_kernel, len(parts)),
        out_shape=[
            jax.ShapeDtypeStruct((num_tok, columns), BF),
            jax.ShapeDtypeStruct((rows, num_tok), BF),
        ],
        in_specs=[vmem] * (len(parts) + 2) + [pl.BlockSpec(memory_space=pl.ANY)] * len(before),
        compiler_params=PARAMS,
        cost_estimate=COST,
    )(*parts, bc_t, tail_t, *before)


def within_kernel(x, bc_t, seg_row, seg_col, run, run_t, step_t, gain, base, grown):
    num_tok, columns = base.shape
    heads = run.shape[1]
    width = columns // heads
    down = lax.broadcasted_iota(jnp.int32, (num_tok, num_tok), 0)
    along = lax.broadcasted_iota(jnp.int32, (num_tok, num_tok), 1)
    keep = (seg_row[...] == seg_col[...]) & (down >= along)
    dim = bc_t.shape[0] // 2
    raw = dot16(bc_t[dim:, :], bc_t[:dim, :], TN)
    scores = jnp.where(keep, raw, 0.0)
    pair = LANES // width
    lane = lax.broadcasted_iota(jnp.int32, (num_tok, LANES), 1) // width
    for first in range(0, heads, pair):
        at = slice(first * width, (first + pair) * width)
        values = x[:, at]
        exact = values.astype(F32)
        total = jnp.zeros((num_tok, LANES), F32)
        rise = jnp.zeros((num_tok, LANES), F32)
        for i in range(pair):
            h = first + i
            run_col = run[:, h : h + 1]
            decay = jnp.exp(jnp.minimum(run_col - run_t[h : h + 1, :], 0.0))
            mixing = (decay * scores * step_t[h : h + 1, :]).astype(BF)
            inner = dot16(mixing, values, NN) + gain[:, h : h + 1] * exact
            total = jnp.where(lane == i, inner, total)
            rise = jnp.where(lane == i, jnp.exp(run_col), rise)
        base[:, at] = total
        grown[:, at] = rise


def within_part(x, bc_t, seg, run, run_t, step_t, gain):
    num_tok, columns = x.shape
    heads = run.shape[1]
    return pl.pallas_call(
        within_kernel,
        out_shape=[jax.ShapeDtypeStruct((num_tok, columns), F32)] * 2,
        compiler_params=PARAMS,
        cost_estimate=COST,
    )(x, bc_t, seg[:, None], seg[None, :], run, run_t, step_t, gain[None])


def outputs_kernel(count, base, grown, *refs):
    held = refs[0][...].astype(F32)
    for block in refs[1:count]:
        held += block[...].astype(F32)
    refs[-1][...] = (base[...] + grown[...] * held).astype(BF)


def outputs_part(base, grown, carried, before):
    vmem = pl.BlockSpec(memory_space=pltpu.VMEM)
    rest = pl.BlockSpec(memory_space=pl.ANY)
    return pl.pallas_call(
        functools.partial(outputs_kernel, len(carried)),
        out_shape=jax.ShapeDtypeStruct(base.shape, BF),
        in_specs=[vmem] * (2 + len(carried)) + [rest] * len(before),
        compiler_params=PARAMS,
        cost_estimate=COST,
    )(base, grown, *carried, *before)


def states_kernel(sources, which, member, state, *refs):
    bundles, (out, done) = refs[:sources], refs[-2:]
    heads, width, dim = state.shape[1:]
    columns = heads * width
    at = pl.program_id(0)
    done[...] = jnp.zeros_like(done)

    def update(bundle):
        b_rows = bundle[columns : columns + dim, :]
        tail = bundle[columns + dim :, :].astype(F32)
        inside = tail[48:49] == member[at].astype(F32)
        weights = jnp.where(inside, tail[:heads], 0.0)
        rise = tail[16 : 16 + heads] + tail[32 : 32 + heads]
        rise = jnp.max(jnp.where(inside, rise, 0.0), axis=1, keepdims=True)
        for h in range(heads):
            rows = slice(h * width, (h + 1) * width)
            scaled = (bundle[rows, :].astype(F32) * weights[h : h + 1]).astype(BF)
            out[0, h] = state[0, h] * rise[h : h + 1] + dot16(scaled, b_rows, NT)

    for i in range(sources):
        pl.when(which[at] == i)(functools.partial(update, bundles[i]))

    @pl.when(which[at] < 0)
    def _():
        out[...] = state[...]


def states_part(which, member, cache, bundles, before):
    slots, heads, width, dim = cache.shape
    rows, num_tok = bundles[0].shape
    slab = pl.BlockSpec((1, heads, width, dim), lambda s, *_: (s, 0, 0, 0))
    fixed = pl.BlockSpec((rows, num_tok), lambda s, *_: (0, 0))
    return pl.pallas_call(
        functools.partial(states_kernel, len(bundles)),
        out_shape=[
            jax.ShapeDtypeStruct(cache.shape, cache.dtype),
            jax.ShapeDtypeStruct((8, LANES), jnp.int32),
        ],
        grid_spec=pltpu.PrefetchScalarGridSpec(
            num_scalar_prefetch=2,
            grid=(slots,),
            in_specs=[slab]
            + [fixed] * len(bundles)
            + [pl.BlockSpec(memory_space=pl.ANY)] * len(before),
            out_specs=[slab, pl.BlockSpec((8, LANES), lambda s, *_: (0, 0))],
        ),
        compiler_params=PARAMS,
        cost_estimate=COST,
    )(which, member, cache, *bundles, *before)


def output_kernel(count, place, w_out, *refs):
    blocks, (kept, given, product) = refs[:count], refs[-3:]
    half = product.shape[0] // 2
    for i, block in enumerate(blocks):
        product[...] = dot16(block[...], w_out[...], NN).astype(BF)
        rows = slice(i * half, (i + 1) * half)
        kept[rows, :] = product[pl.ds(pl.multiple_of(place[1] * half, half), half), :]
        given[rows, :] = product[pl.ds(pl.multiple_of((1 - place[1]) * half, half), half), :]


def output_part(place, w_out, blocks, before):
    vmem = pl.BlockSpec(memory_space=pltpu.VMEM)
    num_tok, columns = blocks[0].shape[0], w_out.shape[1]
    half = jax.ShapeDtypeStruct((len(blocks) * num_tok // 2, columns), BF)
    return pl.pallas_call(
        functools.partial(output_kernel, len(blocks)),
        out_shape=[half, half],
        in_specs=[pl.BlockSpec(memory_space=pltpu.SMEM)]
        + [vmem] * (1 + len(blocks))
        + [pl.BlockSpec(memory_space=pl.ANY)] * len(before),
        scratch_shapes=[pltpu.VMEM((num_tok, columns), BF)],
        compiler_params=PARAMS,
        cost_estimate=COST,
    )(place, w_out, *blocks, *before)


def core_kernel(count, half, place, kept, got, *refs):
    mine, *theirs, total = refs
    chips = 1 + len(theirs)
    share = half // chips
    total[...] = (kept[...].astype(F32) + got[...].astype(F32)).astype(BF)
    for turn, out in enumerate((mine, *theirs)):
        at = lax.rem(place[0] + turn, chips) * share
        for i in range(count):
            rows = pl.ds(pl.multiple_of(i * half + at, share), share)
            out[i * share : (i + 1) * share, :] = total[rows, :]


def core_part(place, kept, got, chips, half):
    vmem = pl.BlockSpec(memory_space=pltpu.VMEM)
    rows, columns = kept.shape
    share = jax.ShapeDtypeStruct((rows // chips, columns), BF)
    mine, *theirs = pl.pallas_call(
        functools.partial(core_kernel, rows // half, half),
        out_shape=[share] * chips,
        in_specs=[pl.BlockSpec(memory_space=pltpu.SMEM), vmem, vmem],
        scratch_shapes=[pltpu.VMEM((rows, columns), BF)],
        compiler_params=PARAMS,
        cost_estimate=COST,
    )(place, kept, got)
    return mine, theirs


def chip_kernel(count, others, mine, *refs):
    theirs, outs = refs[:others], refs[-count:]
    share = mine.shape[0] // count
    for i, out in enumerate(outs):
        rows = slice(i * share, (i + 1) * share)
        total = mine[rows, :].astype(F32)
        for block in theirs:
            total += block[rows, :].astype(F32)
        out[...] = total.astype(BF)


def chip_part(mine, theirs, count, before):
    rows, columns = mine.shape
    vmem = pl.BlockSpec(memory_space=pltpu.VMEM)
    return pl.pallas_call(
        functools.partial(chip_kernel, count, len(theirs)),
        out_shape=[jax.ShapeDtypeStruct((rows // count, columns), BF)] * count,
        in_specs=[vmem] * (1 + len(theirs)) + [pl.BlockSpec(memory_space=pl.ANY)] * len(before),
        compiler_params=PARAMS,
        cost_estimate=COST,
    )(mine, *theirs, *before)


def hold_kernel(count, *refs):
    for source, out in zip(refs[:count], refs[-count:]):
        out[...] = source[...]


def hold_part(arrays, before):
    vmem = pl.BlockSpec(memory_space=pltpu.VMEM)
    return pl.pallas_call(
        functools.partial(hold_kernel, len(arrays)),
        out_shape=[jax.ShapeDtypeStruct(x.shape, x.dtype) for x in arrays],
        in_specs=[vmem] * len(arrays) + [pl.BlockSpec(memory_space=pl.ANY)] * len(before),
        compiler_params=PARAMS,
        cost_estimate=COST,
    )(*arrays, *before)


def order_kernel(count, place, *refs):
    out = refs[-1]
    rows = refs[0].shape[0]
    for k in range(count):
        source = lax.rem(place[4] - k + count, count)
        at = (lax.rem(source, 2) * (count // 2) + lax.div(source, 2)) * rows
        out[pl.ds(pl.multiple_of(at, rows), rows), :] = refs[k][...]


def order_part(place, shares):
    vmem = pl.BlockSpec(memory_space=pltpu.VMEM)
    rows, columns = shares[0].shape
    return pl.pallas_call(
        functools.partial(order_kernel, len(shares)),
        out_shape=jax.ShapeDtypeStruct((rows * len(shares), columns), BF),
        in_specs=[pl.BlockSpec(memory_space=pltpu.SMEM)] + [vmem] * len(shares),
        compiler_params=PARAMS,
        cost_estimate=COST,
    )(place, *shares)


def body(
    tokens,
    w_x,
    w_bc,
    w_dt,
    dt_bias,
    decay_rate,
    skip_gain,
    w_out,
    suffix_lengths,
    checkpoint_slot,
    cache,
):
    reqs = lax.axis_size("req")
    tensors = lax.axis_size("tensor")
    chips = tensors // 2
    own_req = lax.axis_index("req")
    own_tensor = lax.axis_index("tensor")
    own_chip = own_tensor // 2
    core = own_tensor % 2
    num_tok = tokens.shape[0]
    depth = w_x.shape[0]
    slots_dev, heads, width, state_dim = cache.shape
    columns = heads * width
    half = depth // 2
    piece = num_tok // chips
    piece = num_tok // chips

    places = jnp.arange(num_tok, dtype=jnp.int32)
    ends = jnp.cumsum(suffix_lengths[0])
    seg = jnp.sum((places[:, None] >= ends[None, :]).astype(jnp.int32), axis=1)

    share = w_bc.shape[1] // tensors
    bc_share = lax.dynamic_slice_in_dim(w_bc, own_tensor * share, share, axis=1)
    w_small = jnp.concatenate(
        [bc_share, w_dt, w_dt, jnp.zeros((depth, LANES - share - 2 * heads), BF)], axis=1
    )
    place = jnp.stack(
        [own_chip, core, 0 * core + share + heads, 0 * core + share + 2 * heads, own_tensor]
    ).astype(jnp.int32)
    own_block = lax.dynamic_slice(tokens, (0, own_req * depth), (num_tok, depth))
    parts = [jnp.dot(own_block, w_x, preferred_element_type=F32).astype(BF)]
    smalls = [jnp.dot(own_block, w_small, preferred_element_type=F32)]
    order = sorted(range(1, reqs), key=lambda k: min(k, reqs - k))
    def token_block(k, first, rows):
        start = ((own_req + k) % reqs) * depth + core * half
        return lax.dynamic_slice(tokens, (first, start), (rows, half))

    arrived = [token_block(k, 0, num_tok) for k in order[:-1]]
    for i in range(1, len(arrived)):
        (arrived[i],) = hold_part(arrived[i : i + 1], [arrived[i - 1]])
    arrived = [turn_req(block, k) for k, block in zip(order, arrived)]
    blocks = []
    for i, (k, near) in enumerate(zip(order, arrived)):
        block, small = block_part(place, w_small, [near], [swap_core(near)], [])
        smalls.append(turn_req(small, -k))
        blocks.append(block)
        if i == 0:
            products = [product_part(block, w_x, [])]
            parts.append(turn_req(products[0], -k))
    near = turn_req(token_block(order[-1], own_chip * piece, piece), order[-1])
    near = [near] + [turn_chip(near, turn) for turn in range(1, chips)]
    far = [swap_core(block) for block in near]
    block, small = block_part(place, w_small, near, far, smalls[1:] + parts[1:2])
    smalls.append(turn_req(small, -order[-1]))
    for k, near in zip(order[1:-1], blocks[1:]):
        products.append(product_part(near, w_x, [small]))
        parts.append(turn_req(products[-1], -k))
    products.append(product_part(block, w_x, smalls[-1:]))
    parts.append(turn_req(products[-1], -order[-1]))

    bc_share, raw_t = fold_part(smalls[0], smalls[1:], share, heads, [*parts[1:-1], products[-1]])
    quarters = [bc_share] + [turn_tensor(bc_share, k) for k in range(1, tensors)]
    bc_t, c_seg, tail_t, run, run_t, step_t = prep(
        place, raw_t, dt_bias, decay_rate, seg, quarters, []
    )
    c_segs = [c_seg] + [turn_req(c_seg, k) for k in range(1, reqs)]
    x, bundle = gather_part(parts, bc_t, tail_t, [])
    below, above = line_gather(bundle)

    per_pair = (slots_dev + reqs - 1) // reqs
    total_reqs = checkpoint_slot.shape[0]
    req_dev = total_reqs // reqs
    holder = checkpoint_slot // slots_dev
    index = jnp.arange(total_reqs, dtype=jnp.int32)
    owner = index // req_dev
    pair_key = holder * reqs + owner
    rank_in_pair = jnp.sum(
        (pair_key[:, None] == pair_key[None, :])
        & (checkpoint_slot[None, :] < checkpoint_slot[:, None]),
        axis=1,
    )
    away = (own_req - owner) % reqs
    pairs = jnp.arange(reqs * per_pair, dtype=jnp.int32)
    match = (holder == own_req)[None, :] & (
        (away * per_pair + rank_in_pair)[None, :] == pairs[:, None]
    )

    def pick(match, values, missing):
        found = jnp.sum(jnp.where(match, values[None, :], 0), axis=1)
        return jnp.where(jnp.any(match, axis=1), found, missing).astype(jnp.int32)

    pair_slot = pick(match, checkpoint_slot % slots_dev, 0)
    pair_member = pick(match, index % req_dev, -1)

    carried = carried_part(pair_slot, pair_member, c_segs, cache, [])

    base, grown = within_part(x, bc_t, seg, run, run_t, step_t, skip_gain)
    outputs = outputs_part(base, grown, line_sum(carried), [below[-1], above[-1]])

    slot_ids = own_req * slots_dev + jnp.arange(slots_dev, dtype=jnp.int32)
    match_slot = checkpoint_slot[None, :] == slot_ids[:, None]
    which = jnp.where(owner <= own_req, own_req - owner, reqs - 1 + owner - own_req)

    def sum_cores(kept, given):
        mine, theirs = core_part(place, kept, swap_core(given), chips, num_tok // 2)
        return mine, [turn_chip(block, turn + 1) for turn, block in enumerate(theirs)]

    far = order[-1]
    came = {k: turn_req(outputs, k) for k in order}
    kept, given = output_part(place, w_out, [outputs, came[far]], [below[-1], above[-1]])
    new_cache, zero = states_part(
        pick(match_slot, which, -1),
        pick(match_slot, index % req_dev, -1),
        cache,
        [bundle, *below, *above],
        [kept],
    )
    arrived = {}
    arrived[0], block = chip_part(*sum_cores(kept, given), 2, [])
    arrived[far] = turn_req(block, -far)
    before = [zero, block]
    for k in order[-2::-1]:
        kept, given = output_part(place, w_out, [came[k]], before)
        returned = [arrived[j] for j in order if j in arrived] if k == order[0] else []
        (block,) = chip_part(*sum_cores(kept, given), 1, returned)
        arrived[k] = turn_req(block, -k)
        before = [block]

    def column_block(req):
        chosen = arrived[0]
        for k in range(1, reqs):
            chosen = jnp.where((req - own_req) % reqs == k, arrived[k], chosen)
        return chosen

    shares = [column_block(own_tensor)]
    for k in range(1, tensors):
        block = column_block((own_tensor + k) % tensors)
        shares.append(
            lax.ppermute(block, "tensor", [(i, (i + k) % tensors) for i in range(tensors)])
        )
    layer_out = order_part(place, shares)
    return (layer_out, new_cache)


def solution(mesh):
    placed = (
        P(("groups", "req"), None),
        P("req", "tensor"),
        P("req", None),
        P("req", "tensor"),
        P("tensor"),
        P("tensor"),
        P("tensor"),
        P("tensor", "req"),
        P(("groups", "req"), None),
        P("groups"),
        P(("groups", "req"), "tensor", None, None),
    )
    return jax.shard_map(
        body,
        mesh=mesh,
        in_specs=placed,
        out_specs=(P(("groups", "req"), "tensor"), P(("groups", "req"), "tensor", None, None)),
        check_vma=False,
    )
```
